32 devices in a mesh: dp: 16 (over z, x, core), fsdp: 2 (over y).
Axes of the slice: x: 2, y: 2, z: 4, core: 2. Of those that a mesh axis runs over, the one named last changes fastest.
Arguments:
- tokens: bfloat16 [6144, 6144], P(('dp', 'fsdp')), may hold values from -6 to 6
- cotangent: bfloat16 [6144, 6144], P(('dp', 'fsdp')), may hold values from -6 to 6
- lengths: int32 [32, 3], P(('dp', 'fsdp')), may hold values from 0 to 80, as said below
- positions: int32 [2, 6144], P(None, ('dp', 'fsdp')), may hold values from 0 to 63, as said below
- weights: bfloat16 [4, 6144, 256], P(None, 'fsdp'), may hold values from -0.078125 to 0.078125
Outputs:
- grad_tokens: bfloat16 [6144, 6144], P(('dp', 'fsdp'))
- weight_grads: float32 [4, 6144, 256], P(None, 'fsdp')
The draws below stay inside these ranges and needn't reach their ends.
Inputs may be any that keep to these rules, and one draw needn't show every extreme that they name: Devices pair up: dp indices i and i + 8 with the same fsdp index. In every pair exactly one device holds more than 112 live patches; its third image is not empty, its first two images together hold at most 112 patches, and its partner's live patches plus that third image are at most 112. No device holds more than 192 live patches; the first pair's heavy device holds exactly 192. Every non-empty image has at least 10 patches; lengths are 0 only in the light device's third slot. `positions`: each image is laid out row by row with a width w of 2 to 64 patches (exactly 64 for images of 80 patches): its patch number k has row k // w and column k % w; padding rows hold 0.
All inputs are finite; a program needn't handle non-finite values.
Results may differ from the reference program's by a relative error of at most 0.015.
Values may be sent and summed in bfloat16 or wider, within the bound.
A program may use at most 128 MiB of HBM per device.

```python
import math
import jax
import jax.numpy as jnp
from jax import lax

D = 6144
HD = 128
H = 2
TOK_DEV = 112
MAXLEN = 80
GRID = 64
MINLEN = 10
CAP = 192
TOTAL = 6144
DEVICES = 32


def make_lengths(key):
    key = jax.random.fold_in(key, 11)
    pair_count = DEVICES // 2
    subkeys = jax.random.split(key, 6)
    moved = jax.random.randint(subkeys[0], (pair_count,), MAXLEN // 2, MAXLEN + 1)
    moved = moved.at[0].set(MAXLEN)
    heavy_rest = jax.random.randint(subkeys[1], (pair_count,), TOK_DEV + 1 - moved, TOK_DEV + 1)
    heavy_rest = heavy_rest.at[0].set(TOK_DEV)
    low_first = jnp.maximum(MINLEN, heavy_rest - MAXLEN)
    high_first = jnp.minimum(MAXLEN, heavy_rest - MINLEN) + 1
    heavy_first = jax.random.randint(subkeys[2], (pair_count,), low_first, high_first)
    heavy_rows = jnp.stack([heavy_first, heavy_rest - heavy_first, moved], axis=1)
    room_left = TOK_DEV - moved
    light_first = jax.random.randint(subkeys[3], (pair_count,), MINLEN, jnp.minimum(MAXLEN, room_left - MINLEN) + 1)
    light_second = jax.random.randint(subkeys[4], (pair_count,), MINLEN, jnp.minimum(MAXLEN, room_left - light_first) + 1)
    light_rows = jnp.stack([light_first, light_second, jnp.zeros_like(light_first)], axis=1)
    upper_heavy = jax.random.randint(subkeys[5], (pair_count,), 0, 2)
    lower_member = jnp.where(upper_heavy[:, None] == 0, heavy_rows, light_rows)
    upper_member = jnp.where(upper_heavy[:, None] == 0, light_rows, heavy_rows)
    both_members = jnp.stack([lower_member, upper_member], axis=0)
    return both_members.reshape(DEVICES, 3).astype(jnp.int32)


def draw_lengths(key, part):
    return make_lengths(key)


def draw_positions(key, part):
    image_lengths = make_lengths(key)
    key = jax.random.fold_in(key, 23)
    width_top = jnp.maximum(jnp.minimum(GRID, image_lengths), 2) + 1
    widths = jax.random.randint(key, (DEVICES, 3), 2, width_top)
    widths = jnp.where(image_lengths == MAXLEN, GRID, widths)
    image_ends = jnp.cumsum(image_lengths, axis=1)
    image_starts = image_ends - image_lengths
    row_number = jnp.arange(CAP, dtype=jnp.int32)
    slot_number = jnp.sum((row_number[None, :, None] >= image_ends[:, None, :]).astype(jnp.int32), axis=2)
    live = slot_number < 3
    safe_slot = jnp.minimum(slot_number, 2)
    start_of = jnp.take_along_axis(image_starts, safe_slot, axis=1)
    width_of = jnp.take_along_axis(widths, safe_slot, axis=1)
    inside = row_number[None, :] - start_of
    row_place = jnp.where(live, inside // width_of, 0)
    col_place = jnp.where(live, inside % width_of, 0)
    return jnp.stack([row_place.reshape(-1), col_place.reshape(-1)], axis=0).astype(jnp.int32)


def with_spikes(entries, key, source, target, shards_of, factor):
    owner, partner = [(jnp.arange(entries.shape[axis_at]) // (entries.shape[axis_at] // shards_of)).reshape([-1 if axis == axis_at else 1 for axis in range(entries.ndim)]) for axis_at in (source, target)]
    chosen = jax.random.permutation(key, shards_of)[partner]
    strong = (owner == chosen) | (owner == (partner + shards_of // 2) % shards_of)
    return jnp.where(strong, factor * entries, entries)


def steps_of(rng, extent, cuts, smallest, largest):
    gain = 1.0
    for position, parts in cuts:
        steps = jax.random.uniform(jax.random.fold_in(jax.random.fold_in(rng, 6), position), (parts,), jnp.float32, smallest / len(cuts), largest / len(cuts))
        gain = gain * jnp.repeat(jnp.exp(steps), extent[position] // parts).reshape((-1,) + (1,) * (len(extent) - 1 - position))
    return gain


def noise(own_key, shape, scale, most, shards=(), kind=jnp.bfloat16):
    result = scale * jax.random.normal(own_key, shape, jnp.float32)
    if shards:
        result = result * steps_of(own_key, shape, shards, -0.22, 0.18)
    return jnp.clip(result, -most, most).astype(kind)


def noise_with(own_key, extent, scale, limit, shards, heavy, kind=jnp.bfloat16):
    array = scale * jax.random.normal(own_key, extent, jnp.float32)
    if shards:
        array = array * steps_of(own_key, extent, shards, -0.22, 0.18)
    return jnp.clip(with_spikes(array, jax.random.fold_in(own_key, 3), *heavy), -limit, limit).astype(kind)


def setup_inputs(seed: int = 0) -> dict:
    seeds = jax.random.split(jax.random.key(seed), 6)
    tokens = noise(seeds[0], (TOTAL, D), 1.0, 6.0, ((0, 32),))
    cotangent = noise_with(seeds[1], (TOTAL, D), 1.0, 6.0, ((0, 32),), (0, 1, 32, 2.75))
    lengths = draw_lengths(jax.random.fold_in(seeds[5], 71), 0)
    positions = draw_positions(jax.random.fold_in(seeds[5], 71), 0)
    weights = noise(seeds[4], (4, D, H * HD), D ** -0.5, 0.078125, ((1, 2),))
    return {"tokens": tokens, "cotangent": cotangent, "lengths": lengths, "positions": positions, "weights": weights}


rope_base = 100.0

def layer_norm(values):
    center = values - lax.optimization_barrier(jnp.mean(values, axis=-1, keepdims=True))
    return center * lax.rsqrt(lax.optimization_barrier(jnp.mean(center * center, axis=-1, keepdims=True)) + 1e-06)

def rotate(values, row_index, col_index):
    quarter = values.shape[-1] // 4
    frequency = rope_base ** (-jnp.arange(quarter, dtype=jnp.float32) / quarter)
    pieces = []
    for offset, where_at in ((0, row_index), (2 * quarter, col_index)):
        angles = where_at.astype(jnp.float32)[:, None, None] * frequency[None, None, :]
        cosine = jnp.cos(angles)
        sine_part = jnp.sin(angles)
        first_half = values[..., offset:offset + quarter]
        second = values[..., offset + quarter:offset + 2 * quarter]
        pieces.append(first_half * cosine - second * sine_part)
        pieces.append(second * cosine + first_half * sine_part)
    return jnp.concatenate(pieces, axis=-1)

def segment_ids(image_lengths, row_count):
    image_ends = jnp.cumsum(image_lengths)
    row_index = jnp.arange(row_count, dtype=jnp.int32)
    slot_number = lax.optimization_barrier(jnp.sum((row_index[:, None] >= image_ends[None, :]).astype(jnp.int32), axis=1))
    return jnp.where(slot_number < image_lengths.shape[0], slot_number, -1).astype(jnp.int32)

def attend(query_lin, key_lin, value_lin, row_index, col_index, segment):
    row_count = query_lin.shape[0]
    score_scale = 1.0 / math.sqrt(HD)
    queries = rotate(layer_norm(query_lin.reshape(row_count, -1, HD)), row_index, col_index).astype(jnp.bfloat16)
    keys_rot = rotate(layer_norm(key_lin.reshape(row_count, -1, HD)), row_index, col_index).astype(jnp.bfloat16)
    values = value_lin.reshape(row_count, -1, HD).astype(jnp.bfloat16)
    scores = jnp.einsum('qhd,khd->hqk', queries.astype(jnp.float32), keys_rot.astype(jnp.float32)) * score_scale
    same = (segment[:, None] == segment[None, :])[None, :, :]
    exponent = jnp.where(same, jnp.exp(scores), jnp.float32(0.0))
    probabilities = (exponent / lax.optimization_barrier(jnp.sum(exponent, axis=-1, keepdims=True))).astype(jnp.bfloat16)
    attended = jnp.einsum('hqk,khd->qhd', probabilities.astype(jnp.float32), values.astype(jnp.float32)).astype(jnp.bfloat16)
    return attended.reshape(row_count, -1)

def one_device(tokens, cotangent, image_lengths, row_index, col_index, weights):
    head_size = weights.shape[-1]
    model_width = weights.shape[1]
    segment = segment_ids(image_lengths, tokens.shape[0])
    grad_out = jnp.where((segment >= 0)[:, None], cotangent, jnp.zeros_like(cotangent))
    source = tokens.astype(jnp.float32)
    normed = layer_norm(source).astype(jnp.bfloat16)
    merged = jnp.transpose(weights[:3], (1, 0, 2)).reshape(model_width, 3 * head_size)
    linear = jnp.dot(normed, merged, preferred_element_type=jnp.float32)
    grad_attn = jnp.dot(grad_out, weights[3], preferred_element_type=jnp.float32).astype(jnp.bfloat16)

    def core(query_in, key_in, value_in):
        return attend(query_in, key_in, value_in, row_index, col_index, segment)
    attended, pullback = jax.vjp(core, linear[:, :head_size], linear[:, head_size:2 * head_size], linear[:, 2 * head_size:])
    grad_query, grad_key, grad_value = pullback(grad_attn)
    grad_linear = jnp.concatenate([grad_query, grad_key, grad_value], axis=1).astype(jnp.bfloat16)
    grad_normed = lax.dot_general(grad_linear, merged, (((1,), (1,)), ((), ())), preferred_element_type=jnp.float32)
    grad_proj = lax.dot_general(normed, grad_linear, (((0,), (0,)), ((), ())), preferred_element_type=jnp.float32)
    grad_output_w = lax.dot_general(grad_out, attended, (((0,), (0,)), ((), ())), preferred_element_type=jnp.float32)
    term_rows = jnp.concatenate([grad_proj, grad_output_w], axis=1)
    unused, norm_pull = jax.vjp(layer_norm, source)
    grad_tokens = norm_pull(grad_normed)[0].astype(jnp.bfloat16)
    return (grad_tokens, term_rows)

def reference(tokens, cotangent, lengths, positions, weights):
    head_size = weights.shape[-1]
    token_blocks = tokens.reshape(DEVICES, CAP, D)
    grad_blocks = cotangent.reshape(DEVICES, CAP, D)
    place_blocks = jnp.transpose(positions.reshape(2, DEVICES, CAP), (1, 0, 2))

    def step(carried, item):
        block_tokens, block_grads, block_lengths, block_places = item
        grad_tokens, term_rows = one_device(block_tokens, block_grads, block_lengths, block_places[0], block_places[1], weights)
        return (carried + term_rows, grad_tokens)
    start_sum = jnp.zeros((D, 4 * head_size), jnp.float32)
    total_sum, grad_all = lax.scan(step, start_sum, (token_blocks, grad_blocks, lengths, place_blocks))
    weight_grads = jnp.transpose(total_sum.reshape(D, 4, head_size), (1, 0, 2))
    return (grad_all.reshape(DEVICES * CAP, D), weight_grads)
```

```python
import math

import jax
import jax.numpy as jnp
from jax import lax
from jax.sharding import PartitionSpec as P

HD = 128


rope_base = 100.0


def layer_norm(values):
    center = values - jnp.mean(values, axis=-1, keepdims=True)
    return center * lax.rsqrt(jnp.mean(center * center, axis=-1, keepdims=True) + 1e-06)


def rotate(values, row_index, col_index):
    quarter = values.shape[-1] // 4
    frequency = rope_base ** (-jnp.arange(quarter, dtype=jnp.float32) / quarter)
    pieces = []
    for offset, where_at in ((0, row_index), (2 * quarter, col_index)):
        angles = where_at.astype(jnp.float32)[:, None, None] * frequency[None, None, :]
        cosine = jnp.cos(angles)
        sine_part = jnp.sin(angles)
        first_half = values[..., offset : offset + quarter]
        second = values[..., offset + quarter : offset + 2 * quarter]
        pieces.append(first_half * cosine - second * sine_part)
        pieces.append(second * cosine + first_half * sine_part)
    return jnp.concatenate(pieces, axis=-1)


def segment_ids(image_lengths, row_count):
    image_ends = jnp.cumsum(image_lengths)
    row_index = jnp.arange(row_count, dtype=jnp.int32)
    slot_number = jnp.sum((row_index[:, None] >= image_ends[None, :]).astype(jnp.int32), axis=1)
    return jnp.where(slot_number < image_lengths.shape[0], slot_number, -1)


def attend(query_lin, key_lin, value_lin, row_index, col_index, segment):
    row_count = query_lin.shape[0]
    score_scale = 1.0 / math.sqrt(HD)
    queries = rotate(layer_norm(query_lin.reshape(row_count, -1, HD)), row_index, col_index).astype(
        jnp.bfloat16
    )
    keys_rot = rotate(layer_norm(key_lin.reshape(row_count, -1, HD)), row_index, col_index).astype(
        jnp.bfloat16
    )
    values = value_lin.reshape(row_count, -1, HD).astype(jnp.bfloat16)
    scores = (
        jnp.einsum("qhd,khd->hqk", queries.astype(jnp.float32), keys_rot.astype(jnp.float32))
        * score_scale
    )
    same = (segment[:, None] == segment[None, :])[None, :, :]
    exponent = jnp.where(same, jnp.exp(scores), jnp.float32(0.0))
    probabilities = (exponent / jnp.sum(exponent, axis=-1, keepdims=True)).astype(jnp.bfloat16)
    attended = jnp.einsum(
        "hqk,khd->qhd", probabilities.astype(jnp.float32), values.astype(jnp.float32)
    ).astype(jnp.bfloat16)
    return attended.reshape(row_count, -1)


def shifted(value, offset):
    count = lax.axis_size("fsdp")
    return lax.ppermute(value, "fsdp", [(i, (i + offset) % count) for i in range(count)])


def part_of(values, index, width):
    return lax.dynamic_slice_in_dim(values, index * width, width, axis=1)


def over_dp(block, bits):
    count = lax.axis_size("dp")
    me = lax.axis_index("dp")
    for bit in bits:
        pairs = [(i, i ^ (1 << bit)) for i in range(count)]
        mine = (me >> bit) & 1
        half = block.shape[0] // 2
        leaving = lax.dynamic_slice_in_dim(block, (1 - mine) * half, half, axis=0)
        kept = lax.dynamic_slice_in_dim(block, mine * half, half, axis=0)
        arrived = lax.ppermute(leaving.astype(jnp.bfloat16), "dp", pairs)
        block = kept + arrived.astype(jnp.float32)
    block = block.astype(jnp.bfloat16)
    for bit in reversed(bits):
        pairs = [(i, i ^ (1 << bit)) for i in range(count)]
        mine = (me >> bit) & 1
        half = block.shape[0]
        arrived = lax.ppermute(block, "dp", pairs)
        whole = jnp.zeros((2 * half, block.shape[1]), block.dtype)
        whole = lax.dynamic_update_slice_in_dim(whole, block, mine * half, axis=0)
        block = lax.dynamic_update_slice_in_dim(whole, arrived, (1 - mine) * half, axis=0)
    return block


def per_device(tokens, cotangent, lengths, positions, weights):
    capacity = tokens.shape[0]
    slab = weights.shape[1]
    head_size = weights.shape[-1]
    count = lax.axis_size("fsdp")
    me = lax.axis_index("fsdp")
    segment = segment_ids(lengths[0], capacity)
    grad_out = jnp.where((segment >= 0)[:, None], cotangent, jnp.zeros_like(cotangent))
    source = tokens.astype(jnp.float32)
    normed = layer_norm(source).astype(jnp.bfloat16)

    grad_parts = [part_of(grad_out, me, slab)]
    norm_parts = [part_of(normed, me, slab)]
    for k in range(1, count):
        peer = (me + k) % count
        grad_parts.append(shifted(part_of(grad_out, peer, slab), k))
        norm_parts.append(shifted(part_of(normed, peer, slab), k))

    def products(norm_part, grad_part):
        pieces = [jnp.dot(norm_part, weights[i], preferred_element_type=jnp.float32) for i in range(3)]
        pieces.append(jnp.dot(grad_part, weights[3], preferred_element_type=jnp.float32))
        return jnp.concatenate(pieces, axis=1)

    linear = products(norm_parts[0], grad_parts[0])
    for k in range(1, count):
        partial = products(norm_parts[k], grad_parts[k]).astype(jnp.bfloat16)
        linear = linear + shifted(partial, -k).astype(jnp.float32)
    grad_attn = linear[:, 3 * head_size :].astype(jnp.bfloat16)

    def core(query_in, key_in, value_in):
        return attend(query_in, key_in, value_in, positions[0], positions[1], segment)

    attended, pullback = jax.vjp(
        core,
        linear[:, :head_size],
        linear[:, head_size : 2 * head_size],
        linear[:, 2 * head_size : 3 * head_size],
    )
    grad_query, grad_key, grad_value = pullback(grad_attn)
    small = jnp.concatenate(
        [grad_query.astype(jnp.bfloat16), grad_key.astype(jnp.bfloat16), grad_value.astype(jnp.bfloat16), attended],
        axis=1,
    )
    small_parts = [small] + [shifted(small, k) for k in range(1, count)]

    def back(small_part):
        total = None
        for i in range(3):
            term = lax.dot_general(
                small_part[:, i * head_size : (i + 1) * head_size],
                weights[i],
                (((1,), (1,)), ((), ())),
                preferred_element_type=jnp.float32,
            )
            total = term if total is None else total + term
        return total.astype(jnp.bfloat16)

    returned = [(me, back(small))]
    for k in range(1, count):
        returned.append(((me + k) % count, shifted(back(small_parts[k]), -k)))

    norm_all = jnp.concatenate(norm_parts, axis=0)
    grad_all = jnp.concatenate(grad_parts, axis=0)
    small_all = jnp.concatenate(small_parts, axis=0)
    terms = [
        lax.dot_general(
            norm_all if i < 3 else grad_all,
            small_all[:, i * head_size : (i + 1) * head_size],
            (((0,), (0,)), ((), ())),
            preferred_element_type=jnp.float32,
        )
        for i in range(4)
    ]
    bits = list(range(lax.axis_size("dp").bit_length() - 1))
    first = over_dp(jnp.concatenate(terms[:2], axis=0), bits)
    second = over_dp(jnp.concatenate(terms[2:], axis=0), bits[:1] + bits[2:] + bits[1:2])

    grad_normed = jnp.zeros(tokens.shape, jnp.bfloat16)
    for place, part in returned:
        grad_normed = lax.dynamic_update_slice_in_dim(grad_normed, part, place * slab, axis=1)
    unused, norm_pull = jax.vjp(layer_norm, source)
    grad_tokens = norm_pull(grad_normed.astype(jnp.float32))[0].astype(jnp.bfloat16)
    weight_grads = jnp.concatenate([first, second], axis=0).reshape(weights.shape).astype(jnp.float32)
    return (grad_tokens, weight_grads)


def solution(mesh):
    return jax.shard_map(
        per_device,
        mesh=mesh,
        in_specs=(
            P(("dp", "fsdp"), None),
            P(("dp", "fsdp"), None),
            P(("dp", "fsdp"), None),
            P(None, ("dp", "fsdp")),
            P(None, "fsdp", None),
        ),
        out_specs=(P(("dp", "fsdp"), None), P(None, "fsdp", None)),
        check_vma=False,
    )
```

```python
import functools
import math

import jax
import jax.numpy as jnp
from jax import lax
from jax.experimental import pallas as pl
from jax.experimental.pallas import tpu as pltpu
from jax.sharding import PartitionSpec as P

HD = 128
TILE = 256


rope_base = 100.0


def layer_norm(values):
    center = values - jnp.mean(values, axis=-1, keepdims=True)
    return center * lax.rsqrt(jnp.mean(center * center, axis=-1, keepdims=True) + 1e-06)


def rotate(values, row_index, col_index):
    quarter = values.shape[-1] // 4
    frequency = rope_base ** (-jnp.arange(quarter, dtype=jnp.float32) / quarter)
    pieces = []
    for offset, where_at in ((0, row_index), (2 * quarter, col_index)):
        angles = where_at.astype(jnp.float32)[:, None, None] * frequency[None, None, :]
        cosine = jnp.cos(angles)
        sine_part = jnp.sin(angles)
        first_half = values[..., offset : offset + quarter]
        second = values[..., offset + quarter : offset + 2 * quarter]
        pieces.append(first_half * cosine - second * sine_part)
        pieces.append(second * cosine + first_half * sine_part)
    return jnp.concatenate(pieces, axis=-1)


def segment_ids(image_lengths, row_count):
    image_ends = jnp.cumsum(image_lengths)
    row_index = jnp.arange(row_count, dtype=jnp.int32)
    slot_number = jnp.sum((row_index[:, None] >= image_ends[None, :]).astype(jnp.int32), axis=1)
    return jnp.where(slot_number < image_lengths.shape[0], slot_number, -1)


def attend(query_lin, key_lin, value_lin, row_index, col_index, segment):
    row_count = query_lin.shape[0]
    score_scale = 1.0 / math.sqrt(HD)
    queries = rotate(layer_norm(query_lin.reshape(row_count, -1, HD)), row_index, col_index).astype(
        jnp.bfloat16
    )
    keys_rot = rotate(layer_norm(key_lin.reshape(row_count, -1, HD)), row_index, col_index).astype(
        jnp.bfloat16
    )
    values = value_lin.reshape(row_count, -1, HD).astype(jnp.bfloat16)
    scores = (
        jnp.einsum("qhd,khd->hqk", queries.astype(jnp.float32), keys_rot.astype(jnp.float32))
        * score_scale
    )
    same = (segment[:, None] == segment[None, :])[None, :, :]
    exponent = jnp.where(same, jnp.exp(scores), jnp.float32(0.0))
    probabilities = (exponent / jnp.sum(exponent, axis=-1, keepdims=True)).astype(jnp.bfloat16)
    attended = jnp.einsum(
        "hqk,khd->qhd", probabilities.astype(jnp.float32), values.astype(jnp.float32)
    ).astype(jnp.bfloat16)
    return attended.reshape(row_count, -1)


def shifted(value, offset):
    count = lax.axis_size("fsdp")
    return lax.ppermute(value, "fsdp", [(i, (i + offset) % count) for i in range(count)])


def part_of(values, index, width):
    return lax.dynamic_slice_in_dim(values, index * width, width, axis=1)


def sum_kernel(orders, slab, head_size, lhs_ref, small_ref, out_ref, acc, outgoing, incoming, send_sem, recv_sem):
    me = lax.axis_index("dp")
    streams, steps = len(orders), len(orders[0])
    rows = 4 * slab // streams
    halves = [rows >> (s + 1) for s in range(steps)]
    starts = [rows - 2 * halves[s] for s in range(steps)]
    bit_of = [(me // (1 << bit)) % 2 for bit in range(steps)]
    peer_of = [me + (1 - 2 * bit_of[bit]) * (1 << bit) for bit in range(steps)]

    barrier = pltpu.get_barrier_semaphore()
    for bit in range(steps):
        pl.semaphore_signal(barrier, inc=1, device_id={"dp": peer_of[bit]}, device_id_type=pl.DeviceIdType.MESH)
    pl.semaphore_wait(barrier, steps)

    def term(stream, row):
        row = stream * rows + row
        weight = row // slab
        left = pl.multiple_of((weight // 3) * slab + row % slab, TILE)
        column = pl.multiple_of(weight * head_size, head_size)
        return jnp.dot(
            lhs_ref[pl.ds(left, TILE), :],
            small_ref[:, pl.ds(column, head_size)],
            preferred_element_type=jnp.float32,
        )

    def exchange(phase, stream, step, source, target):
        copy = pltpu.make_async_remote_copy(
            src_ref=source,
            dst_ref=target,
            send_sem=send_sem.at[phase, stream, step],
            recv_sem=recv_sem.at[phase, stream, step],
            device_id={"dp": peer_of[orders[stream][step]]},
            device_id_type=pl.DeviceIdType.MESH,
        )
        copy.start()
        return copy

    copies = {}
    offsets = {}
    for stream in range(streams):
        half = halves[0]
        mine = bit_of[orders[stream][0]]

        @pl.loop(0, half // TILE)
        def leaving(t):
            value = term(stream, (1 - mine) * half + t * TILE)
            outgoing[stream, pl.ds(pl.multiple_of(t * TILE, TILE), TILE), :] = value.astype(jnp.bfloat16)

        copies[0, stream, 0] = exchange(
            0, stream, 0, outgoing.at[stream, pl.ds(0, half)], incoming.at[stream, pl.ds(0, half)]
        )
        offsets[stream, 0] = mine * half

    for stream in range(streams):
        half = halves[0]
        mine = bit_of[orders[stream][0]]

        @pl.loop(0, half // TILE)
        def kept(t):
            acc[stream, pl.ds(pl.multiple_of(t * TILE, TILE), TILE), :] = term(stream, mine * half + t * TILE)

    for step in range(1, steps + 1):
        for stream in range(streams):
            copies[0, stream, step - 1].wait_recv()
            got = starts[step - 1]
            base = offsets[stream, step - 1] - offsets[stream, 0]
            if step < steps:
                half = halves[step]
                size = min(half, 192)
                mine = bit_of[orders[stream][step]]
                go, stay = (1 - mine) * half, mine * half

                @pl.loop(0, half // size)
                def leaving(t):
                    at = pl.multiple_of(t * size, size)
                    value = acc[stream, pl.ds(pl.multiple_of(base + go + at, size), size), :]
                    other = incoming[stream, pl.ds(pl.multiple_of(got + go + at, size), size), :]
                    outgoing[stream, pl.ds(pl.multiple_of(starts[step] + at, size), size), :] = (
                        value + other.astype(jnp.float32)
                    ).astype(jnp.bfloat16)

                place = pl.ds(starts[step], half)
                copies[0, stream, step] = exchange(
                    0, stream, step, outgoing.at[stream, place], incoming.at[stream, place]
                )

                @pl.loop(0, half // size)
                def kept(t):
                    at = pl.multiple_of(t * size, size)
                    where = pl.ds(pl.multiple_of(base + stay + at, size), size)
                    other = incoming[stream, pl.ds(pl.multiple_of(got + stay + at, size), size), :]
                    acc[stream, where, :] = acc[stream, where, :] + other.astype(jnp.float32)

                offsets[stream, step] = offsets[stream, step - 1] + stay
            else:
                half = halves[steps - 1]
                place = pl.ds(pl.multiple_of(stream * rows + offsets[stream, steps - 1], half), half)
                value = acc[stream, pl.ds(pl.multiple_of(base, half), half), :]
                other = incoming[stream, pl.ds(got, half), :]
                out_ref[place, :] = (value + other.astype(jnp.float32)).astype(jnp.bfloat16)
                copies[1, stream, steps - 1] = exchange(
                    1, stream, steps - 1, out_ref.at[place], out_ref.at[place]
                )

    for step in reversed(range(steps - 1)):
        for stream in range(streams):
            copies[1, stream, step + 1].wait_recv()
            half = halves[step]
            place = pl.ds(pl.multiple_of(stream * rows + offsets[stream, step], half), half)
            copies[1, stream, step] = exchange(1, stream, step, out_ref.at[place], out_ref.at[place])
    for stream in range(streams):
        copies[1, stream, 0].wait_recv()
    for copy in copies.values():
        copy.wait_send()


def summed_terms(lhs, small, slab, head_size):
    steps = lax.axis_size("dp").bit_length() - 1
    streams = 4 if (slab >> steps) % 16 == 0 else 2
    rows = 4 * slab // streams
    plain = list(range(steps))
    turned = plain[:1] + plain[2:] + plain[1:2]
    orders = [turned] + [plain] * (streams - 1)
    moved = rows - (rows >> steps)
    return pl.pallas_call(
        functools.partial(sum_kernel, orders, slab, head_size),
        out_shape=jax.ShapeDtypeStruct((4 * slab, head_size), jnp.bfloat16),
        in_specs=[pl.BlockSpec(memory_space=pltpu.VMEM)] * 2,
        out_specs=pl.BlockSpec(memory_space=pltpu.VMEM),
        scratch_shapes=[
            pltpu.VMEM((streams, rows // 2, head_size), jnp.float32),
            pltpu.VMEM((streams, moved, head_size), jnp.bfloat16),
            pltpu.VMEM((streams, moved, head_size), jnp.bfloat16),
            pltpu.SemaphoreType.DMA((2, streams, steps)),
            pltpu.SemaphoreType.DMA((2, streams, steps)),
        ],
        compiler_params=pltpu.CompilerParams(
            collective_id=0, has_side_effects=True, vmem_limit_bytes=48 * 1024 * 1024
        ),
        cost_estimate=pl.CostEstimate(flops=10**9, bytes_accessed=10**8, transcendentals=0),
    )(lhs, small)


def per_device(tokens, cotangent, lengths, positions, weights):
    capacity = tokens.shape[0]
    slab = weights.shape[1]
    head_size = weights.shape[-1]
    count = lax.axis_size("fsdp")
    me = lax.axis_index("fsdp")
    segment = segment_ids(lengths[0], capacity)
    grad_out = jnp.where((segment >= 0)[:, None], cotangent, jnp.zeros_like(cotangent))
    source = tokens.astype(jnp.float32)
    normed = layer_norm(source).astype(jnp.bfloat16)

    grad_parts = [part_of(grad_out, me, slab)]
    norm_parts = [part_of(normed, me, slab)]
    for k in range(1, count):
        peer = (me + k) % count
        grad_parts.append(shifted(part_of(grad_out, peer, slab), k))
        norm_parts.append(shifted(part_of(normed, peer, slab), k))

    def products(norm_part, grad_part):
        pieces = [jnp.dot(norm_part, weights[i], preferred_element_type=jnp.float32) for i in range(3)]
        pieces.append(jnp.dot(grad_part, weights[3], preferred_element_type=jnp.float32))
        return jnp.concatenate(pieces, axis=1)

    linear = products(norm_parts[0], grad_parts[0])
    for k in range(1, count):
        partial = products(norm_parts[k], grad_parts[k]).astype(jnp.bfloat16)
        linear = linear + shifted(partial, -k).astype(jnp.float32)
    grad_attn = linear[:, 3 * head_size :].astype(jnp.bfloat16)

    def core(query_in, key_in, value_in):
        return attend(query_in, key_in, value_in, positions[0], positions[1], segment)

    attended, pullback = jax.vjp(
        core,
        linear[:, :head_size],
        linear[:, head_size : 2 * head_size],
        linear[:, 2 * head_size : 3 * head_size],
    )
    grad_query, grad_key, grad_value = pullback(grad_attn)
    small = jnp.concatenate(
        [grad_query.astype(jnp.bfloat16), grad_key.astype(jnp.bfloat16), grad_value.astype(jnp.bfloat16), attended],
        axis=1,
    )
    small_parts = [small] + [shifted(small, k) for k in range(1, count)]

    def back(small_part):
        total = None
        for i in range(3):
            term = lax.dot_general(
                small_part[:, i * head_size : (i + 1) * head_size],
                weights[i],
                (((1,), (1,)), ((), ())),
                preferred_element_type=jnp.float32,
            )
            total = term if total is None else total + term
        return total.astype(jnp.bfloat16)

    returned = [(me, back(small))]
    for k in range(1, count):
        returned.append(((me + k) % count, shifted(back(small_parts[k]), -k)))

    norm_all = jnp.concatenate(norm_parts, axis=0)
    grad_all = jnp.concatenate(grad_parts, axis=0)
    small_all = jnp.concatenate(small_parts, axis=0)
    lhs = jnp.concatenate([norm_all.T, grad_all.T], axis=0)
    summed = summed_terms(lhs, small_all, slab, head_size)

    grad_normed = jnp.zeros(tokens.shape, jnp.bfloat16)
    for place, part in returned:
        grad_normed = lax.dynamic_update_slice_in_dim(grad_normed, part, place * slab, axis=1)
    unused, norm_pull = jax.vjp(layer_norm, source)
    grad_tokens = norm_pull(grad_normed.astype(jnp.float32))[0].astype(jnp.bfloat16)
    weight_grads = summed.reshape(weights.shape).astype(jnp.float32)
    return (grad_tokens, weight_grads)


def solution(mesh):
    return jax.shard_map(
        per_device,
        mesh=mesh,
        in_specs=(
            P(("dp", "fsdp"), None),
            P(("dp", "fsdp"), None),
            P(("dp", "fsdp"), None),
            P(None, ("dp", "fsdp")),
            P(None, "fsdp", None),
        ),
        out_specs=(P(("dp", "fsdp"), None), P(None, "fsdp", None)),
        check_vma=False,
    )
```

```python
import functools
import math

import jax
import jax.numpy as jnp
from jax import lax
from jax.experimental import pallas as pl
from jax.experimental.pallas import tpu as pltpu
from jax.sharding import PartitionSpec as P

HD = 128
TILE = 256

EPS = 1e-06
rope_base = 100.0


def side_tables(lengths, positions, capacity):
    ends = [lengths[0, 0], lengths[0, 0] + lengths[0, 1], lengths[0, 0] + lengths[0, 1] + lengths[0, 2]]

    def slots(rows):
        slot = sum((rows >= end).astype(jnp.float32) for end in ends)
        return jnp.where(slot < 3, slot, -1.0)

    column = slots(lax.broadcasted_iota(jnp.int32, (capacity, 1), 0))
    line = slots(lax.broadcasted_iota(jnp.int32, (8, capacity), 1))
    lane = lax.broadcasted_iota(jnp.int32, (capacity, HD), 1)
    quarter = HD // 4
    frequency = rope_base ** (-(lane % quarter).astype(jnp.float32) / quarter)
    place = jnp.where(lane < HD // 2, positions[0][:, None], positions[1][:, None]).astype(jnp.float32)
    angles = place * frequency
    sign = jnp.where((lane // quarter) % 2 == 0, -1.0, 1.0)
    return column, line, jnp.cos(angles), sign * jnp.sin(angles)


def normalize(values):
    center = values - jnp.mean(values, axis=-1, keepdims=True)
    scale = lax.rsqrt(jnp.mean(center * center, axis=-1, keepdims=True) + EPS)
    return center * scale, scale


def normalize_back(grad, normal, scale):
    inner = jnp.mean(grad * normal, axis=-1, keepdims=True)
    return scale * (grad - jnp.mean(grad, axis=-1, keepdims=True) - normal * inner)


def swap_quarters(values):
    quarter = HD // 4
    lane = lax.broadcasted_iota(jnp.int32, values.shape, 1)
    return jnp.where(
        (lane // quarter) % 2 == 0, pltpu.roll(values, HD - quarter, 1), pltpu.roll(values, quarter, 1)
    )


def dot(left, right):
    return jnp.dot(left, right, preferred_element_type=jnp.float32)


def dot_nt(left, right):
    return lax.dot_general(left, right, (((1,), (1,)), ((), ())), preferred_element_type=jnp.float32)


def layer_kernel(
    orders, tokens_ref, cot_ref, column_ref, line_ref, cos_ref, sin_ref, weights_hbm, out_ref, tokens_out,
    weights, normed, gout, norm_in, gout_in, mean_ref, scale_ref, linear, lin_send, lin_in, attn_send, attn_in,
    lhs_ref, small, back, back_send, acc, outgoing, incoming, w_sem, y_send, y_recv, send_sem, recv_sem,
):
    capacity = tokens_ref.shape[0]
    slab, head_size = weights.shape[1], weights.shape[2]
    shards = normed.shape[0]
    heads = head_size // HD
    me = lax.axis_index("dp")
    shard = lax.axis_index("fsdp")
    streams, steps = len(orders), len(orders[0])
    rows = 4 * slab // streams
    halves = [rows >> (s + 1) for s in range(steps)]
    starts = [rows - 2 * halves[s] for s in range(steps)]
    bit_of = [(me // (1 << bit)) % 2 for bit in range(steps)]
    peer_of = [me + (1 - 2 * bit_of[bit]) * (1 << bit) for bit in range(steps)]
    others = range(1, shards)

    fetch = pltpu.make_async_copy(weights_hbm, weights, w_sem)
    fetch.start()
    barrier = pltpu.get_barrier_semaphore()
    for bit in range(steps):
        pl.semaphore_signal(barrier, inc=1, device_id={"dp": peer_of[bit]}, device_id_type=pl.DeviceIdType.MESH)
    for k in others:
        pl.semaphore_signal(
            barrier, inc=1, device_id={"fsdp": (shard + k) % shards}, device_id_type=pl.DeviceIdType.MESH
        )

    started = []

    def across(kind, k, direction, source, target):
        copy = pltpu.make_async_remote_copy(
            src_ref=source,
            dst_ref=target,
            send_sem=y_send.at[kind, k],
            recv_sem=y_recv.at[kind, k],
            device_id={"fsdp": (shard + shards + direction * k) % shards},
            device_id_type=pl.DeviceIdType.MESH,
        )
        copy.start()
        started.append(copy)
        return copy

    chunk = capacity // 2
    parts = [pl.ds(0, chunk), pl.ds(chunk, chunk)]
    group = 16

    def mask_cotangent(part):
        @pl.loop(0, chunk // group)
        def masked(t):
            at = pl.ds(pl.multiple_of(part * chunk + t * group, group), group)
            live = (column_ref[at, :] >= 0).astype(jnp.float32)
            for p in range(shards):
                value = cot_ref[at, p * slab : (p + 1) * slab].astype(jnp.float32)
                gout[p, at, :] = (value * live).astype(jnp.bfloat16)

    def normalize_tokens(part):
        @pl.loop(0, chunk // group)
        def normal(t):
            at = pl.ds(pl.multiple_of(part * chunk + t * group, group), group)
            value = tokens_ref[at, :].astype(jnp.float32)
            mean = jnp.mean(value, axis=-1, keepdims=True)
            center = value - mean
            scale = lax.rsqrt(jnp.mean(center * center, axis=-1, keepdims=True) + EPS)
            mean_ref[at, :] = jnp.broadcast_to(mean, (group, HD))
            scale_ref[at, :] = jnp.broadcast_to(scale, (group, HD))
            result = (center * scale).astype(jnp.bfloat16)
            for p in range(shards):
                normed[p, at, :] = result[:, p * slab : (p + 1) * slab]

    gout_copies, norm_copies = {}, {}

    def send_gout(part):
        for k in others:
            gout_copies[part, k] = across(
                part, k, 1, gout.at[(shard + k) % shards, parts[part]], gout_in.at[k - 1, parts[part]]
            )

    def send_norm(part):
        for k in others:
            norm_copies[part, k] = across(
                2 + part, k, 1, normed.at[(shard + k) % shards, parts[part]], norm_in.at[k - 1, parts[part]]
            )

    mask_cotangent(0)
    pl.semaphore_wait(barrier, steps + shards - 1)
    send_gout(0)
    normalize_tokens(0)
    send_norm(0)
    normalize_tokens(1)
    send_norm(1)
    mask_cotangent(1)
    send_gout(1)

    fetch.wait()
    for i in range(3):
        linear[:, i * head_size : (i + 1) * head_size] = dot(normed[shard], weights[i])
    linear[:, 3 * head_size :] = dot(gout[shard], weights[3])

    lin_copies, attn_copies = {}, {}

    def attn_partial(part):
        for k in others:
            gout_copies[part, k].wait_recv()
            attn_send[k - 1, parts[part], :] = dot(gout_in[k - 1, parts[part], :], weights[3]).astype(jnp.bfloat16)
            attn_copies[part, k] = across(
                4 + part, k, -1, attn_send.at[k - 1, parts[part]], attn_in.at[k - 1, parts[part]]
            )

    def lin_partial(part):
        for k in others:
            norm_copies[part, k].wait_recv()
            for i in range(3):
                lin_send[k - 1, parts[part], i * head_size : (i + 1) * head_size] = dot(
                    norm_in[k - 1, parts[part], :], weights[i]
                ).astype(jnp.bfloat16)
            lin_copies[part, k] = across(
                6 + part, k, -1, lin_send.at[k - 1, parts[part]], lin_in.at[k - 1, parts[part]]
            )

    attn_partial(0)
    lin_partial(0)
    lin_partial(1)

    def transpose_into(base, own, arrived):
        @pl.loop(0, slab // TILE)
        def turn(t):
            at = pl.ds(pl.multiple_of(t * TILE, TILE), TILE)
            whole = jnp.concatenate([own[shard, :, at]] + [arrived[k - 1, :, at] for k in others], axis=0)
            lhs_ref[pl.ds(pl.multiple_of(base + t * TILE, TILE), TILE), :] = whole.T

    transpose_into(0, normed, norm_in)
    for part in range(2):
        for k in others:
            lin_copies[part, k].wait_recv()
            linear[parts[part], : 3 * head_size] += lin_in[k - 1, parts[part], :].astype(jnp.float32)

    cosine, sine = cos_ref[...], sin_ref[...]
    same = column_ref[...] == line_ref[0:1, :]
    score_scale = 1.0 / math.sqrt(HD)
    saved = []
    for h in range(heads):
        normals = []
        turned = []
        for which in range(2):
            first = which * head_size + h * HD
            normal, scale = normalize(linear[:, first : first + HD])
            normals.append((normal, scale))
            turned.append((normal * cosine + swap_quarters(normal) * sine).astype(jnp.bfloat16))
        first = 2 * head_size + h * HD
        values = linear[:, first : first + HD].astype(jnp.bfloat16)
        queries, keys = turned
        exponent = jnp.where(same, jnp.exp(dot_nt(queries, keys) * score_scale), 0.0)
        prob = exponent / jnp.sum(exponent, axis=1, keepdims=True)
        exponent = jnp.where(same, jnp.exp(dot_nt(keys, queries) * score_scale), 0.0)
        prob_t = exponent / jnp.sum(exponent, axis=0, keepdims=True)
        small[3, 0:capacity, h * HD : (h + 1) * HD] = dot(prob.astype(jnp.bfloat16), values).astype(jnp.bfloat16)
        saved.append((normals, queries, keys, values, prob, prob_t))
    arrivals = [
        across(8, k, 1, small.at[3, pl.ds(0, capacity)], small.at[3, pl.ds(k * capacity, capacity)]) for k in others
    ]

    attn_partial(1)
    transpose_into(slab, gout, gout_in)
    for part in range(2):
        for k in others:
            attn_copies[part, k].wait_recv()
            linear[parts[part], 3 * head_size :] += attn_in[k - 1, parts[part], :].astype(jnp.float32)

    for h in range(heads):
        normals, queries, keys, values, prob, prob_t = saved[h]
        first = 3 * head_size + h * HD
        grad = linear[:, first : first + HD].astype(jnp.bfloat16)
        grad_prob = dot_nt(grad, values).astype(jnp.bfloat16).astype(jnp.float32)
        grad_score = prob * (grad_prob - jnp.sum(grad_prob * prob, axis=1, keepdims=True)) * score_scale
        grad_prob = dot_nt(values, grad).astype(jnp.bfloat16).astype(jnp.float32)
        grad_score_t = prob_t * (grad_prob - jnp.sum(grad_prob * prob_t, axis=0, keepdims=True)) * score_scale
        gradients = [
            dot(grad_score.astype(jnp.bfloat16), keys),
            dot(grad_score_t.astype(jnp.bfloat16), queries),
        ]
        place = slice(h * HD, (h + 1) * HD)
        for which in range(2):
            gradient = gradients[which].astype(jnp.bfloat16).astype(jnp.float32)
            gradient = gradient * cosine + swap_quarters(gradient * sine)
            small[which, 0:capacity, place] = normalize_back(gradient, *normals[which]).astype(jnp.bfloat16)
        small[2, 0:capacity, place] = dot(prob_t.astype(jnp.bfloat16), grad).astype(jnp.bfloat16)
    arrivals += [
        across(
            9, k, 1, small.at[pl.ds(0, 3), pl.ds(0, capacity)], small.at[pl.ds(0, 3), pl.ds(k * capacity, capacity)]
        )
        for k in others
    ]

    def slice_gradient(slot, store):
        @pl.loop(0, slab // TILE)
        def tile(t):
            at = pl.ds(pl.multiple_of(t * TILE, TILE), TILE)
            total = sum(
                dot_nt(small[i, slot * capacity : (slot + 1) * capacity, :], weights[i, at, :]) for i in range(3)
            )
            store(at, total.astype(jnp.bfloat16))

    def own_slice(at, value):
        back[shard, :, at] = value

    slice_gradient(0, own_slice)
    for copy in arrivals:
        copy.wait_recv()

    back_copies = []

    def return_gradients():
        for k in others:

            def keep(at, value):
                back_send[k - 1, :, at] = value

            slice_gradient(k, keep)
            back_copies.append(across(10, k, -1, back_send.at[k - 1], back.at[shard]))

    def token_gradients():
        for copy in back_copies:
            copy.wait_recv()

        @pl.loop(0, capacity // group)
        def piece(t):
            at = pl.ds(pl.multiple_of(t * group, group), group)
            scale = scale_ref[at, 0:1]
            normal = (tokens_ref[at, :].astype(jnp.float32) - mean_ref[at, 0:1]) * scale
            grad = jnp.concatenate([back[p, at, :] for p in range(shards)], axis=1).astype(jnp.float32)
            tokens_out[at, :] = normalize_back(grad, normal, scale).astype(jnp.bfloat16)

    def term(stream, row):
        row = stream * rows + row
        weight = row // slab
        left = pl.multiple_of((weight // 3) * slab + row % slab, TILE)
        return dot(lhs_ref[pl.ds(left, TILE), :], small[weight])

    def exchange(phase, stream, step, source, target):
        copy = pltpu.make_async_remote_copy(
            src_ref=source,
            dst_ref=target,
            send_sem=send_sem.at[phase, stream, step],
            recv_sem=recv_sem.at[phase, stream, step],
            device_id={"dp": peer_of[orders[stream][step]]},
            device_id_type=pl.DeviceIdType.MESH,
        )
        copy.start()
        return copy

    copies = {}
    offsets = {}
    for stream in range(streams):
        half = halves[0]
        mine = bit_of[orders[stream][0]]

        @pl.loop(0, half // TILE)
        def leaving(t):
            value = term(stream, (1 - mine) * half + t * TILE)
            outgoing[stream, pl.ds(pl.multiple_of(t * TILE, TILE), TILE), :] = value.astype(jnp.bfloat16)

        copies[0, stream, 0] = exchange(
            0, stream, 0, outgoing.at[stream, pl.ds(0, half)], incoming.at[stream, pl.ds(0, half)]
        )
        offsets[stream, 0] = mine * half

    for stream in range(streams):
        half = halves[0]
        mine = bit_of[orders[stream][0]]

        @pl.loop(0, half // TILE)
        def kept(t):
            acc[stream, pl.ds(pl.multiple_of(t * TILE, TILE), TILE), :] = term(stream, mine * half + t * TILE)

    return_gradients()

    for step in range(1, steps + 1):
        for stream in range(streams):
            copies[0, stream, step - 1].wait_recv()
            got = starts[step - 1]
            base = offsets[stream, step - 1] - offsets[stream, 0]
            if step < steps:
                half = halves[step]
                size = min(half, 192)
                mine = bit_of[orders[stream][step]]
                go, stay = (1 - mine) * half, mine * half

                @pl.loop(0, half // size)
                def leaving(t):
                    at = pl.multiple_of(t * size, size)
                    value = acc[stream, pl.ds(pl.multiple_of(base + go + at, size), size), :]
                    other = incoming[stream, pl.ds(pl.multiple_of(got + go + at, size), size), :]
                    outgoing[stream, pl.ds(pl.multiple_of(starts[step] + at, size), size), :] = (
                        value + other.astype(jnp.float32)
                    ).astype(jnp.bfloat16)

                place = pl.ds(starts[step], half)
                copies[0, stream, step] = exchange(
                    0, stream, step, outgoing.at[stream, place], incoming.at[stream, place]
                )

                @pl.loop(0, half // size)
                def kept(t):
                    at = pl.multiple_of(t * size, size)
                    where = pl.ds(pl.multiple_of(base + stay + at, size), size)
                    other = incoming[stream, pl.ds(pl.multiple_of(got + stay + at, size), size), :]
                    acc[stream, where, :] = acc[stream, where, :] + other.astype(jnp.float32)

                offsets[stream, step] = offsets[stream, step - 1] + stay
            else:
                half = halves[steps - 1]
                place = pl.ds(pl.multiple_of(stream * rows + offsets[stream, steps - 1], half), half)
                value = acc[stream, pl.ds(pl.multiple_of(base, half), half), :]
                other = incoming[stream, pl.ds(got, half), :]
                out_ref[place, :] = (value + other.astype(jnp.float32)).astype(jnp.bfloat16)
                copies[1, stream, steps - 1] = exchange(
                    1, stream, steps - 1, out_ref.at[place], out_ref.at[place]
                )

    token_gradients()

    for step in reversed(range(steps - 1)):
        for stream in range(streams):
            copies[1, stream, step + 1].wait_recv()
            half = halves[step]
            place = pl.ds(pl.multiple_of(stream * rows + offsets[stream, step], half), half)
            copies[1, stream, step] = exchange(1, stream, step, out_ref.at[place], out_ref.at[place])
    for stream in range(streams):
        copies[1, stream, 0].wait_recv()
    for copy in copies.values():
        copy.wait_send()
    for copy in started:
        copy.wait_send()


def per_device(tokens, cotangent, lengths, positions, weights):
    capacity, width = tokens.shape
    slab, head_size = weights.shape[1:]
    shards = lax.axis_size("fsdp")
    steps = lax.axis_size("dp").bit_length() - 1
    streams = 4 if (slab >> steps) % 16 == 0 else 2
    rows = 4 * slab // streams
    plain = list(range(steps))
    turned = plain[:1] + plain[2:] + plain[1:2]
    orders = [turned] + [plain] * (streams - 1)
    moved = rows - (rows >> steps)
    column, line, cosine, sine = side_tables(lengths, positions, capacity)
    vmem = pl.BlockSpec(memory_space=pltpu.VMEM)
    half = jnp.bfloat16
    summed, grad_tokens = pl.pallas_call(
        functools.partial(layer_kernel, orders),
        out_shape=(
            jax.ShapeDtypeStruct((4 * slab, head_size), half),
            jax.ShapeDtypeStruct((capacity, width), half),
        ),
        in_specs=[vmem] * 6 + [pl.BlockSpec(memory_space=pl.ANY)],
        out_specs=(vmem, vmem),
        scratch_shapes=[
            pltpu.VMEM((4, slab, head_size), half),
            pltpu.VMEM((shards, capacity, slab), half),
            pltpu.VMEM((shards, capacity, slab), half),
            pltpu.VMEM((shards - 1, capacity, slab), half),
            pltpu.VMEM((shards - 1, capacity, slab), half),
            pltpu.VMEM((capacity, HD), jnp.float32),
            pltpu.VMEM((capacity, HD), jnp.float32),
            pltpu.VMEM((capacity, 4 * head_size), jnp.float32),
            pltpu.VMEM((shards - 1, capacity, 3 * head_size), half),
            pltpu.VMEM((shards - 1, capacity, 3 * head_size), half),
            pltpu.VMEM((shards - 1, capacity, head_size), half),
            pltpu.VMEM((shards - 1, capacity, head_size), half),
            pltpu.VMEM((2 * slab, shards * capacity), half),
            pltpu.VMEM((4, shards * capacity, head_size), half),
            pltpu.VMEM((shards, capacity, slab), half),
            pltpu.VMEM((shards - 1, capacity, slab), half),
            pltpu.VMEM((streams, rows // 2, head_size), jnp.float32),
            pltpu.VMEM((streams, moved, head_size), half),
            pltpu.VMEM((streams, moved, head_size), half),
            pltpu.SemaphoreType.DMA,
            pltpu.SemaphoreType.DMA((11, shards)),
            pltpu.SemaphoreType.DMA((11, shards)),
            pltpu.SemaphoreType.DMA((2, streams, steps)),
            pltpu.SemaphoreType.DMA((2, streams, steps)),
        ],
        compiler_params=pltpu.CompilerParams(
            collective_id=0, has_side_effects=True, vmem_limit_bytes=62 * 1024 * 1024
        ),
        cost_estimate=pl.CostEstimate(flops=4 * 10**9, bytes_accessed=10**8, transcendentals=10**5),
    )(tokens, cotangent, column, line, cosine, sine, weights)
    return (grad_tokens, summed.reshape(weights.shape).astype(jnp.float32))


def solution(mesh):
    return jax.shard_map(
        per_device,
        mesh=mesh,
        in_specs=(
            P(("dp", "fsdp"), None),
            P(("dp", "fsdp"), None),
            P(("dp", "fsdp"), None),
            P(None, ("dp", "fsdp")),
            P(None, "fsdp", None),
        ),
        out_specs=(P(("dp", "fsdp"), None), P(None, "fsdp", None)),
        check_vma=False,
    )
```

```python
import functools
import math

import jax
import jax.numpy as jnp
from jax import lax
from jax.experimental import pallas as pl
from jax.experimental.pallas import tpu as pltpu
from jax.sharding import PartitionSpec as P

HD = 128
TILE = 256

EPS = 1e-06
rope_base = 100.0


def segment_slots(lengths_ref, rows):
    end = 0
    slot = jnp.zeros(rows.shape, jnp.float32)
    for image in range(3):
        end = end + lengths_ref[0, image]
        slot = slot + jnp.where(rows >= end, 1.0, 0.0)
    return jnp.where(slot < 3.0, slot, -1.0)


def rotary_tables(positions_ref):
    capacity = positions_ref.shape[1]
    down = lax.broadcasted_iota(jnp.int32, (capacity, capacity), 0)
    along = lax.broadcasted_iota(jnp.int32, (capacity, capacity), 1)

    def column(i):
        line = positions_ref[i : i + 1, :].astype(jnp.float32)
        return jnp.sum(jnp.where(down == along, line, 0.0), axis=1, keepdims=True)

    lane = lax.broadcasted_iota(jnp.int32, (capacity, HD), 1)
    quarter = HD // 4
    frequency = jnp.exp((lane % quarter).astype(jnp.float32) * (-math.log(rope_base) / quarter))
    angles = jnp.where(lane < HD // 2, column(0), column(1)) * frequency
    sign = jnp.where((lane // quarter) % 2 == 0, -1.0, 1.0)
    return jnp.cos(angles), sign * jnp.sin(angles)


def exchange_plan(orders, halves):
    streams, steps = len(orders), len(halves)
    stages = [(0, s) for s in range(steps)] + [(1, s) for s in reversed(range(steps))]
    link = lambda bit: min(bit, 2)
    busy = {0: 0.0, 1: 0.0, 2: 0.0}
    flying = {0: 0, 1: 0, 2: 0}
    waiting = {0: [], 1: [], 2: []}
    depth = {0: streams, 1: 2, 2: 2}
    events, plan = [], []

    def launch(now, stream, place):
        step = stages[place][1]
        bit = orders[stream][step]
        kind = link(bit)
        if flying[kind] >= depth[kind]:
            waiting[kind].append((stream, place))
            return
        flying[kind] += 1
        cost = halves[step] * 0.0114 * (0.2 if bit == 0 else 1.0 if bit < 3 else 1.4)
        busy[kind] = max(busy[kind], now) + cost
        events.append((busy[kind] + 1.0, stream, place, kind))
        plan.append(("start", stream) + stages[place] + (now,))

    for stream in range(streams):
        launch(1.0 * stream, stream, 0)
    now = 0.0
    while events:
        event = min(events)
        events.remove(event)
        when, stream, place, kind = event
        now = max(now + 0.3, when)
        plan.append(("wait", stream) + stages[place] + (now,))
        flying[kind] -= 1
        if waiting[kind]:
            launch(now, *waiting[kind].pop(0))
        if place + 1 < len(stages):
            launch(now, stream, place + 1)
    return plan


def normalize(values):
    center = values - jnp.mean(values, axis=-1, keepdims=True)
    scale = lax.rsqrt(jnp.mean(center * center, axis=-1, keepdims=True) + EPS)
    return center * scale, scale


def normalize_back(grad, normal, scale):
    inner = jnp.mean(grad * normal, axis=-1, keepdims=True)
    return scale * (grad - jnp.mean(grad, axis=-1, keepdims=True) - normal * inner)


def swap_quarters(values):
    quarter = HD // 4
    lane = lax.broadcasted_iota(jnp.int32, values.shape, 1)
    return jnp.where(
        (lane // quarter) % 2 == 0, pltpu.roll(values, HD - quarter, 1), pltpu.roll(values, quarter, 1)
    )


def dot(left, right):
    return jnp.dot(left, right, preferred_element_type=jnp.float32)


def dot_nt(left, right):
    return lax.dot_general(left, right, (((1,), (1,)), ((), ())), preferred_element_type=jnp.float32)


def layer_kernel(
    orders, tokens_ref, cot_ref, lengths_ref, positions_ref, weights_hbm, out_ref, tokens_out,
    weights, normed, gout, norm_in, gout_in, mean_ref, scale_ref, linear, lin_send, lin_in, attn_send, attn_in,
    lhs_ref, small, back, back_send, acc, outgoing, incoming, w_sem, y_send, y_recv, send_sem, recv_sem,
):
    capacity = tokens_ref.shape[0]
    slab, head_size = weights.shape[1], weights.shape[2]
    shards = normed.shape[0]
    heads = head_size // HD
    me = lax.axis_index("dp")
    shard = lax.axis_index("fsdp")
    streams, steps = len(orders), len(orders[0])
    rows = 4 * slab // streams
    halves = [rows >> (s + 1) for s in range(steps)]
    starts = [rows - 2 * halves[s] for s in range(steps)]
    bit_of = [(me // (1 << bit)) % 2 for bit in range(steps)]
    peer_of = [me + (1 - 2 * bit_of[bit]) * (1 << bit) for bit in range(steps)]
    others = range(1, shards)
    plan = exchange_plan(orders, halves)

    fetch = pltpu.make_async_copy(weights_hbm, weights, w_sem)
    fetch.start()
    barrier = pltpu.get_barrier_semaphore()
    for bit in range(steps):
        pl.semaphore_signal(barrier, inc=1, device_id={"dp": peer_of[bit]}, device_id_type=pl.DeviceIdType.MESH)
    for k in others:
        pl.semaphore_signal(
            barrier, inc=1, device_id={"fsdp": (shard + k) % shards}, device_id_type=pl.DeviceIdType.MESH
        )

    started = []

    def across(kind, k, direction, source, target):
        copy = pltpu.make_async_remote_copy(
            src_ref=source,
            dst_ref=target,
            send_sem=y_send.at[kind, k],
            recv_sem=y_recv.at[kind, k],
            device_id={"fsdp": (shard + shards + direction * k) % shards},
            device_id_type=pl.DeviceIdType.MESH,
        )
        copy.start()
        started.append(copy)
        return copy

    chunk = capacity // 2
    parts = [pl.ds(0, chunk), pl.ds(chunk, chunk)]
    group = 16

    def mask_cotangent(part):
        @pl.loop(0, chunk // group)
        def masked(t):
            at = pl.ds(pl.multiple_of(part * chunk + t * group, group), group)
            row = part * chunk + t * group + lax.broadcasted_iota(jnp.int32, (group, 1), 0)
            live = jnp.where(segment_slots(lengths_ref, row) >= 0.0, 1.0, 0.0)
            for p in range(shards):
                value = cot_ref[at, p * slab : (p + 1) * slab].astype(jnp.float32)
                gout[p, at, :] = (value * live).astype(jnp.bfloat16)

    def normalize_tokens(part):
        @pl.loop(0, chunk // group)
        def normal(t):
            at = pl.ds(pl.multiple_of(part * chunk + t * group, group), group)
            value = tokens_ref[at, :].astype(jnp.float32)
            mean = jnp.mean(value, axis=-1, keepdims=True)
            center = value - mean
            scale = lax.rsqrt(jnp.mean(center * center, axis=-1, keepdims=True) + EPS)
            mean_ref[at, :] = jnp.broadcast_to(mean, (group, HD))
            scale_ref[at, :] = jnp.broadcast_to(scale, (group, HD))
            result = (center * scale).astype(jnp.bfloat16)
            for p in range(shards):
                normed[p, at, :] = result[:, p * slab : (p + 1) * slab]

    gout_copies, norm_copies = {}, {}

    def send_gout(part):
        for k in others:
            gout_copies[part, k] = across(
                part, k, 1, gout.at[(shard + k) % shards, parts[part]], gout_in.at[k - 1, parts[part]]
            )

    def send_norm(part):
        for k in others:
            norm_copies[part, k] = across(
                2 + part, k, 1, normed.at[(shard + k) % shards, parts[part]], norm_in.at[k - 1, parts[part]]
            )

    mask_cotangent(0)
    pl.semaphore_wait(barrier, steps + shards - 1)
    send_gout(0)
    normalize_tokens(0)
    send_norm(0)
    normalize_tokens(1)
    send_norm(1)
    mask_cotangent(1)
    send_gout(1)

    fetch.wait()
    for i in range(3):
        linear[:, i * head_size : (i + 1) * head_size] = dot(normed[shard], weights[i])
    linear[:, 3 * head_size :] = dot(gout[shard], weights[3])

    cosine, sine = rotary_tables(positions_ref)
    lin_copies, attn_copies = {}, {}

    def attn_partial(part):
        for k in others:
            gout_copies[part, k].wait_recv()
            attn_send[k - 1, parts[part], :] = dot(gout_in[k - 1, parts[part], :], weights[3]).astype(jnp.bfloat16)
            attn_copies[part, k] = across(
                4 + part, k, -1, attn_send.at[k - 1, parts[part]], attn_in.at[k - 1, parts[part]]
            )

    def lin_partial(part):
        for k in others:
            norm_copies[part, k].wait_recv()
            for i in range(3):
                lin_send[k - 1, parts[part], i * head_size : (i + 1) * head_size] = dot(
                    norm_in[k - 1, parts[part], :], weights[i]
                ).astype(jnp.bfloat16)
            lin_copies[part, k] = across(
                6 + part, k, -1, lin_send.at[k - 1, parts[part]], lin_in.at[k - 1, parts[part]]
            )

    attn_partial(0)
    lin_partial(0)
    lin_partial(1)

    def transpose_into(base, own, arrived):
        @pl.loop(0, slab // TILE)
        def turn(t):
            at = pl.ds(pl.multiple_of(t * TILE, TILE), TILE)
            whole = jnp.concatenate([own[shard, :, at]] + [arrived[k - 1, :, at] for k in others], axis=0)
            lhs_ref[pl.ds(pl.multiple_of(base + t * TILE, TILE), TILE), :] = whole.T

    transpose_into(0, normed, norm_in)
    for part in range(2):
        for k in others:
            lin_copies[part, k].wait_recv()
            linear[parts[part], : 3 * head_size] += lin_in[k - 1, parts[part], :].astype(jnp.float32)

    same = segment_slots(lengths_ref, lax.broadcasted_iota(jnp.int32, (capacity, 1), 0)) == segment_slots(
        lengths_ref, lax.broadcasted_iota(jnp.int32, (1, capacity), 1)
    )
    score_scale = 1.0 / math.sqrt(HD)
    saved = []
    for h in range(heads):
        normals = []
        turned = []
        for which in range(2):
            first = which * head_size + h * HD
            normal, scale = normalize(linear[:, first : first + HD])
            normals.append((normal, scale))
            turned.append((normal * cosine + swap_quarters(normal) * sine).astype(jnp.bfloat16))
        first = 2 * head_size + h * HD
        values = linear[:, first : first + HD].astype(jnp.bfloat16)
        queries, keys = turned
        exponent = jnp.where(same, jnp.exp(dot_nt(queries, keys) * score_scale), 0.0)
        prob = exponent / jnp.sum(exponent, axis=1, keepdims=True)
        exponent = jnp.where(same, jnp.exp(dot_nt(keys, queries) * score_scale), 0.0)
        prob_t = exponent / jnp.sum(exponent, axis=0, keepdims=True)
        small[3, 0:capacity, h * HD : (h + 1) * HD] = dot(prob.astype(jnp.bfloat16), values).astype(jnp.bfloat16)
        saved.append((normals, queries, keys, values, prob, prob_t))
    arrivals = [
        across(8, k, 1, small.at[3, pl.ds(0, capacity)], small.at[3, pl.ds(k * capacity, capacity)]) for k in others
    ]

    attn_partial(1)
    transpose_into(slab, gout, gout_in)
    for part in range(2):
        for k in others:
            attn_copies[part, k].wait_recv()
            linear[parts[part], 3 * head_size :] += attn_in[k - 1, parts[part], :].astype(jnp.float32)

    for h in range(heads):
        normals, queries, keys, values, prob, prob_t = saved[h]
        first = 3 * head_size + h * HD
        grad = linear[:, first : first + HD].astype(jnp.bfloat16)
        grad_prob = dot_nt(grad, values).astype(jnp.bfloat16).astype(jnp.float32)
        grad_score = prob * (grad_prob - jnp.sum(grad_prob * prob, axis=1, keepdims=True)) * score_scale
        grad_prob = dot_nt(values, grad).astype(jnp.bfloat16).astype(jnp.float32)
        grad_score_t = prob_t * (grad_prob - jnp.sum(grad_prob * prob_t, axis=0, keepdims=True)) * score_scale
        gradients = [
            dot(grad_score.astype(jnp.bfloat16), keys),
            dot(grad_score_t.astype(jnp.bfloat16), queries),
        ]
        place = slice(h * HD, (h + 1) * HD)
        for which in range(2):
            gradient = gradients[which].astype(jnp.bfloat16).astype(jnp.float32)
            gradient = gradient * cosine + swap_quarters(gradient * sine)
            small[which, 0:capacity, place] = normalize_back(gradient, *normals[which]).astype(jnp.bfloat16)
        small[2, 0:capacity, place] = dot(prob_t.astype(jnp.bfloat16), grad).astype(jnp.bfloat16)
    arrivals += [
        across(
            9, k, 1, small.at[pl.ds(0, 3), pl.ds(0, capacity)], small.at[pl.ds(0, 3), pl.ds(k * capacity, capacity)]
        )
        for k in others
    ]

    def slice_gradient(slot, store):
        @pl.loop(0, slab // TILE)
        def tile(t):
            at = pl.ds(pl.multiple_of(t * TILE, TILE), TILE)
            total = sum(
                dot_nt(small[i, slot * capacity : (slot + 1) * capacity, :], weights[i, at, :]) for i in range(3)
            )
            store(at, total.astype(jnp.bfloat16))

    def own_slice(at, value):
        back[shard, :, at] = value

    slice_gradient(0, own_slice)
    for copy in arrivals:
        copy.wait_recv()

    back_copies = []

    def return_gradients():
        for k in others:

            def keep(at, value):
                back_send[k - 1, :, at] = value

            slice_gradient(k, keep)
            back_copies.append(across(10, k, -1, back_send.at[k - 1], back.at[shard]))

    def token_gradients(number):
        if number == 0:
            for copy in back_copies:
                copy.wait_recv()

        @pl.loop(0, chunk // 2 // group)
        def piece(t):
            at = pl.ds(pl.multiple_of(number * (chunk // 2) + t * group, group), group)
            scale = scale_ref[at, 0:1]
            normal = (tokens_ref[at, :].astype(jnp.float32) - mean_ref[at, 0:1]) * scale
            grad = jnp.concatenate([back[p, at, :] for p in range(shards)], axis=1).astype(jnp.float32)
            tokens_out[at, :] = normalize_back(grad, normal, scale).astype(jnp.bfloat16)

    def term(stream, row):
        row = stream * rows + row
        weight = row // slab
        left = pl.multiple_of((weight // 3) * slab + row % slab, TILE)
        return dot(lhs_ref[pl.ds(left, TILE), :], small[weight])

    def exchange(phase, stream, step, source, target):
        copy = pltpu.make_async_remote_copy(
            src_ref=source,
            dst_ref=target,
            send_sem=send_sem.at[phase, stream, step],
            recv_sem=recv_sem.at[phase, stream, step],
            device_id={"dp": peer_of[orders[stream][step]]},
            device_id_type=pl.DeviceIdType.MESH,
        )
        copy.start()
        return copy

    copies = {}
    offsets = {}
    for stream in range(streams):
        half = halves[0]
        mine = bit_of[orders[stream][0]]

        @pl.loop(0, half // TILE)
        def leaving(t):
            value = term(stream, (1 - mine) * half + t * TILE)
            outgoing[stream, pl.ds(pl.multiple_of(t * TILE, TILE), TILE), :] = value.astype(jnp.bfloat16)

        copies[0, stream, 0] = exchange(
            0, stream, 0, outgoing.at[stream, pl.ds(0, half)], incoming.at[stream, pl.ds(0, half)]
        )
        offsets[stream, 0] = mine * half

    for stream in range(streams):
        half = halves[0]
        mine = bit_of[orders[stream][0]]

        @pl.loop(0, half // TILE)
        def kept(t):
            acc[stream, pl.ds(pl.multiple_of(t * TILE, TILE), TILE), :] = term(stream, mine * half + t * TILE)

    def combine(stream, step):
        copies[0, stream, step - 1].wait_recv()
        got = starts[step - 1]
        base = offsets[stream, step - 1] - offsets[stream, 0]
        if step == steps:
            half = halves[steps - 1]
            place = pl.ds(pl.multiple_of(stream * rows + offsets[stream, steps - 1], half), half)
            value = acc[stream, pl.ds(pl.multiple_of(base, half), half), :]
            other = incoming[stream, pl.ds(got, half), :]
            out_ref[place, :] = (value + other.astype(jnp.float32)).astype(jnp.bfloat16)
            return
        half = halves[step]
        size = min(half, 192)
        mine = bit_of[orders[stream][step]]
        go, stay = (1 - mine) * half, mine * half

        @pl.loop(0, half // size)
        def leaving(t):
            at = pl.multiple_of(t * size, size)
            value = acc[stream, pl.ds(pl.multiple_of(base + go + at, size), size), :]
            other = incoming[stream, pl.ds(pl.multiple_of(got + go + at, size), size), :]
            outgoing[stream, pl.ds(pl.multiple_of(starts[step] + at, size), size), :] = (
                value + other.astype(jnp.float32)
            ).astype(jnp.bfloat16)

        offsets[stream, step] = offsets[stream, step - 1] + stay

    def combine_kept(stream, step):
        got = starts[step - 1]
        base = offsets[stream, step - 1] - offsets[stream, 0]
        half = halves[step]
        size = min(half, 192)
        stay = bit_of[orders[stream][step]] * half

        @pl.loop(0, half // size)
        def kept(t):
            at = pl.multiple_of(t * size, size)
            where = pl.ds(pl.multiple_of(base + stay + at, size), size)
            other = incoming[stream, pl.ds(pl.multiple_of(got + stay + at, size), size), :]
            acc[stream, where, :] = acc[stream, where, :] + other.astype(jnp.float32)

    return_gradients()
    finish = plan[-1][-1]
    pieces = [(0.5 + 0.1 * number) * finish for number in range(4)]
    behind = []
    for action, stream, phase, step, when in plan:
        if action == "start":
            if phase == 0 and step == 0:
                continue
            if phase == 0:
                place = pl.ds(starts[step], halves[step])
                source, target = outgoing.at[stream, place], incoming.at[stream, place]
            else:
                place = pl.ds(pl.multiple_of(stream * rows + offsets[stream, step], halves[step]), halves[step])
                source, target = out_ref.at[place], out_ref.at[place]
            copies[phase, stream, step] = exchange(phase, stream, step, source, target)
        else:
            for job in behind:
                combine_kept(*job)
            behind = []
            while pieces and when > pieces[0]:
                token_gradients(4 - len(pieces))
                pieces.pop(0)
            if phase == 0:
                combine(stream, step + 1)
                if step + 1 < steps:
                    behind.append((stream, step + 1))
            else:
                copies[phase, stream, step].wait_recv()
    for copy in copies.values():
        copy.wait_send()
    for copy in started:
        copy.wait_send()


def per_device(tokens, cotangent, lengths, positions, weights):
    capacity, width = tokens.shape
    slab, head_size = weights.shape[1:]
    shards = lax.axis_size("fsdp")
    steps = lax.axis_size("dp").bit_length() - 1
    streams = next(n for n in (8, 4, 2, 1) if (4 * slab // n >> steps) % 16 == 0)
    rows = 4 * slab // streams
    plain = list(range(steps))
    turned = plain[:1] + plain[2:] + plain[1:2]
    orders = [turned] * (streams // 8) + [plain] * (streams - streams // 8)
    moved = rows - (rows >> steps)
    vmem = pl.BlockSpec(memory_space=pltpu.VMEM)
    half = jnp.bfloat16
    summed, grad_tokens = pl.pallas_call(
        functools.partial(layer_kernel, orders),
        out_shape=(
            jax.ShapeDtypeStruct((4 * slab, head_size), half),
            jax.ShapeDtypeStruct((capacity, width), half),
        ),
        in_specs=[vmem, vmem, pl.BlockSpec(memory_space=pltpu.SMEM), vmem, pl.BlockSpec(memory_space=pl.ANY)],
        out_specs=(vmem, vmem),
        scratch_shapes=[
            pltpu.VMEM((4, slab, head_size), half),
            pltpu.VMEM((shards, capacity, slab), half),
            pltpu.VMEM((shards, capacity, slab), half),
            pltpu.VMEM((shards - 1, capacity, slab), half),
            pltpu.VMEM((shards - 1, capacity, slab), half),
            pltpu.VMEM((capacity, HD), jnp.float32),
            pltpu.VMEM((capacity, HD), jnp.float32),
            pltpu.VMEM((capacity, 4 * head_size), jnp.float32),
            pltpu.VMEM((shards - 1, capacity, 3 * head_size), half),
            pltpu.VMEM((shards - 1, capacity, 3 * head_size), half),
            pltpu.VMEM((shards - 1, capacity, head_size), half),
            pltpu.VMEM((shards - 1, capacity, head_size), half),
            pltpu.VMEM((2 * slab, shards * capacity), half),
            pltpu.VMEM((4, shards * capacity, head_size), half),
            pltpu.VMEM((shards, capacity, slab), half),
            pltpu.VMEM((shards - 1, capacity, slab), half),
            pltpu.VMEM((streams, rows // 2, head_size), jnp.float32),
            pltpu.VMEM((streams, moved, head_size), half),
            pltpu.VMEM((streams, moved, head_size), half),
            pltpu.SemaphoreType.DMA,
            pltpu.SemaphoreType.DMA((11, shards)),
            pltpu.SemaphoreType.DMA((11, shards)),
            pltpu.SemaphoreType.DMA((2, streams, steps)),
            pltpu.SemaphoreType.DMA((2, streams, steps)),
        ],
        compiler_params=pltpu.CompilerParams(
            collective_id=0, has_side_effects=True, vmem_limit_bytes=62 * 1024 * 1024
        ),
        cost_estimate=pl.CostEstimate(flops=4 * 10**9, bytes_accessed=10**8, transcendentals=10**5),
    )(tokens, cotangent, lengths, positions, weights)
    return (grad_tokens, summed.reshape(weights.shape).astype(jnp.float32))


def solution(mesh):
    return jax.shard_map(
        per_device,
        mesh=mesh,
        in_specs=(
            P(("dp", "fsdp"), None),
            P(("dp", "fsdp"), None),
            P(("dp", "fsdp"), None),
            P(None, ("dp", "fsdp")),
            P(None, "fsdp", None),
        ),
        out_specs=(P(("dp", "fsdp"), None), P(None, "fsdp", None)),
        check_vma=False,
    )
```

```python
import functools
import math

import jax
import jax.numpy as jnp
from jax import lax
from jax.experimental import pallas as pl
from jax.experimental.pallas import tpu as pltpu
from jax.sharding import PartitionSpec as P

HD = 128
TILE = 384
CORES = 2

EPS = 1e-06
rope_base = 100.0


def segment_slots(lengths_ref, rows):
    end = 0
    slot = jnp.zeros(rows.shape, jnp.float32)
    for image in range(3):
        end = end + lengths_ref[0, image]
        slot = slot + jnp.where(rows >= end, 1.0, 0.0)
    return jnp.where(slot < 3.0, slot, -1.0)


def rotary_tables(positions_ref):
    capacity = positions_ref.shape[1]
    down = lax.broadcasted_iota(jnp.int32, (capacity, capacity), 0)
    along = lax.broadcasted_iota(jnp.int32, (capacity, capacity), 1)

    def column(i):
        line = positions_ref[i : i + 1, :].astype(jnp.float32)
        return jnp.sum(jnp.where(down == along, line, 0.0), axis=1, keepdims=True)

    lane = lax.broadcasted_iota(jnp.int32, (capacity, HD), 1)
    quarter = HD // 4
    frequency = jnp.exp((lane % quarter).astype(jnp.float32) * (-math.log(rope_base) / quarter))
    angles = jnp.where(lane < HD // 2, column(0), column(1)) * frequency
    sign = jnp.where((lane // quarter) % 2 == 0, -1.0, 1.0)
    return jnp.cos(angles), sign * jnp.sin(angles)


def exchange_plan(orders, halves):
    streams, steps = len(orders), len(halves)
    stages = [(0, s) for s in range(steps)] + [(1, s) for s in reversed(range(steps))] + [(1, steps)]
    busy, flying, waiting = [0.0] * 4, [0] * 4, [[], [], [], []]
    price = [0.25, 1.0, 1.0, 2.0]
    events, plan = [], []

    def launch(now, stream, place):
        step = stages[place][1]
        kind = min(orders[stream][step], 3) if step < steps else 0
        if flying[kind] >= 3:
            waiting[kind].append((stream, place))
            return
        flying[kind] += 1
        size = halves[step] if step < steps else 2 * halves[0]
        busy[kind] = max(busy[kind], now) + size * 0.0114 * price[kind]
        events.append((busy[kind] + 1.0, stream, place, kind))
        plan.append(("start", stream) + stages[place] + (now,))

    for stream in range(streams):
        launch(0.7 * stream, stream, 0)
    now = 0.0
    while events:
        event = min(events)
        events.remove(event)
        when, stream, place, kind = event
        now = max(now + 0.3, when)
        plan.append(("wait", stream) + stages[place] + (now,))
        flying[kind] -= 1
        if waiting[kind]:
            launch(now, *waiting[kind].pop(0))
        if place + 1 < len(stages):
            launch(now, stream, place + 1)
    return plan


def normalize(values):
    center = values - jnp.mean(values, axis=-1, keepdims=True)
    scale = lax.rsqrt(jnp.mean(center * center, axis=-1, keepdims=True) + EPS)
    return center * scale, scale


def normalize_back(grad, normal, scale):
    inner = jnp.mean(grad * normal, axis=-1, keepdims=True)
    return scale * (grad - jnp.mean(grad, axis=-1, keepdims=True) - normal * inner)


def swap_quarters(values):
    quarter = HD // 4
    lane = lax.broadcasted_iota(jnp.int32, values.shape, 1)
    return jnp.where(
        (lane // quarter) % 2 == 0, pltpu.roll(values, HD - quarter, 1), pltpu.roll(values, quarter, 1)
    )


def dot(left, right):
    return jnp.dot(left, right, preferred_element_type=jnp.float32)


def dot_nt(left, right):
    return lax.dot_general(left, right, (((1,), (1,)), ((), ())), preferred_element_type=jnp.float32)


def layer_kernel(
    orders, tokens_ref, cot_ref, lengths_ref, positions_ref, weights_hbm, out_ref, tokens_out,
    weights, normed, gout, norm_in, gout_in, mean_ref, scale_ref, linear, lin_send, lin_in, attn_send, attn_in,
    lhs_ref, small, back, back_send, acc, outgoing, incoming, w_sem, y_send, y_recv, send_sem, recv_sem,
):
    capacity = tokens_ref.shape[0]
    slab, head_size = weights.shape[1], weights.shape[2]
    shards = normed.shape[0]
    heads = head_size // HD
    me = lax.axis_index("dp")
    core = me % CORES
    shard = lax.axis_index("fsdp") * CORES + core
    streams, steps = len(orders), len(orders[0])
    rows = 4 * slab // streams
    halves = [rows >> (s + 1) for s in range(steps)]
    starts = [rows - 2 * halves[s] for s in range(steps)]
    bit_of = [(me // (1 << bit)) % 2 for bit in range(steps + 1)]
    peer_of = [me + (1 - 2 * bit_of[bit]) * (1 << bit) for bit in range(steps + 1)]
    others = range(1, shards)
    plan = exchange_plan(orders, halves)

    def member(offset):
        index = (shard + shards + offset) % shards
        return {"dp": me - core + index % CORES, "fsdp": index // CORES}

    fetch = pltpu.make_async_copy(weights_hbm.at[:, pl.ds(pl.multiple_of(core * slab, slab), slab)], weights, w_sem)
    fetch.start()
    barrier = pltpu.get_barrier_semaphore()
    for bit in range(1, steps + 1):
        pl.semaphore_signal(barrier, inc=1, device_id={"dp": peer_of[bit]}, device_id_type=pl.DeviceIdType.MESH)
    for k in others:
        pl.semaphore_signal(barrier, inc=1, device_id=member(k), device_id_type=pl.DeviceIdType.MESH)

    started = []

    def across(kind, k, direction, source, target):
        copy = pltpu.make_async_remote_copy(
            src_ref=source,
            dst_ref=target,
            send_sem=y_send.at[kind, k],
            recv_sem=y_recv.at[kind, k],
            device_id=member(direction * k),
            device_id_type=pl.DeviceIdType.MESH,
        )
        copy.start()
        started.append(copy)
        return copy

    chunk = capacity // 2
    parts = [pl.ds(0, chunk), pl.ds(chunk, chunk)]
    group = 16

    def mask_cotangent(part):
        @pl.loop(0, chunk // group)
        def masked(t):
            at = pl.ds(pl.multiple_of(part * chunk + t * group, group), group)
            row = part * chunk + t * group + lax.broadcasted_iota(jnp.int32, (group, 1), 0)
            live = jnp.where(segment_slots(lengths_ref, row) >= 0.0, 1.0, 0.0)
            for p in range(shards):
                value = cot_ref[at, p * slab : (p + 1) * slab].astype(jnp.float32)
                gout[p, at, :] = (value * live).astype(jnp.bfloat16)

    def normalize_tokens(part):
        @pl.loop(0, chunk // group)
        def normal(t):
            at = pl.ds(pl.multiple_of(part * chunk + t * group, group), group)
            value = tokens_ref[at, :].astype(jnp.float32)
            mean = jnp.mean(value, axis=-1, keepdims=True)
            center = value - mean
            scale = lax.rsqrt(jnp.mean(center * center, axis=-1, keepdims=True) + EPS)
            mean_ref[at, :] = jnp.broadcast_to(mean, (group, HD))
            scale_ref[at, :] = jnp.broadcast_to(scale, (group, HD))
            result = (center * scale).astype(jnp.bfloat16)
            for p in range(shards):
                normed[p, at, :] = result[:, p * slab : (p + 1) * slab]

    gout_copies, norm_copies = {}, {}

    def send_gout(part):
        for k in others:
            gout_copies[part, k] = across(
                part, k, 1, gout.at[(shard + k) % shards, parts[part]], gout_in.at[part, k - 1]
            )

    def send_norm(part):
        for k in others:
            norm_copies[part, k] = across(
                2 + part, k, 1, normed.at[(shard + k) % shards, parts[part]], norm_in.at[part, k - 1]
            )

    mask_cotangent(0)
    pl.semaphore_wait(barrier, steps + shards - 1)
    send_gout(0)
    normalize_tokens(0)
    send_norm(0)
    normalize_tokens(1)
    send_norm(1)
    mask_cotangent(1)
    send_gout(1)

    fetch.wait()
    for i in range(3):
        linear[:, i * head_size : (i + 1) * head_size] = dot(normed[shard], weights[i])
    linear[:, 3 * head_size :] = dot(gout[shard], weights[3])

    cosine, sine = rotary_tables(positions_ref)
    lin_copies, attn_copies = {}, {}

    apart = (shards - 1, chunk, -1)
    joined = ((shards - 1) * chunk, slab)

    def attn_partial(part):
        for k in others:
            gout_copies[part, k].wait_recv()
        partial = dot(gout_in[part].reshape(joined), weights[3])
        attn_send[part] = partial.astype(jnp.bfloat16).reshape(apart)
        for k in others:
            attn_copies[part, k] = across(4 + part, k, -1, attn_send.at[part, k - 1], attn_in.at[part, k - 1])

    def lin_partial(part):
        for k in others:
            norm_copies[part, k].wait_recv()
        for i in range(3):
            partial = dot(norm_in[part].reshape(joined), weights[i])
            lin_send[part, :, :, i * head_size : (i + 1) * head_size] = partial.astype(jnp.bfloat16).reshape(apart)
        for k in others:
            lin_copies[part, k] = across(6 + part, k, -1, lin_send.at[part, k - 1], lin_in.at[part, k - 1])

    attn_partial(0)
    lin_partial(0)
    lin_partial(1)

    def transpose_into(base, own, arrived):
        @pl.loop(0, slab // TILE)
        def turn(t):
            at = pl.ds(pl.multiple_of(t * TILE, TILE), TILE)
            whole = jnp.concatenate([own[shard, :, at]] + [arrived[part, k - 1, :, at] for k in others for part in range(2)], axis=0)
            lhs_ref[pl.ds(pl.multiple_of(base + t * TILE, TILE), TILE), :] = whole.T

    transpose_into(0, normed, norm_in)
    for part in range(2):
        for k in others:
            lin_copies[part, k].wait_recv()
            linear[parts[part], : 3 * head_size] += lin_in[part, k - 1].astype(jnp.float32)

    same = segment_slots(lengths_ref, lax.broadcasted_iota(jnp.int32, (capacity, 1), 0)) == segment_slots(
        lengths_ref, lax.broadcasted_iota(jnp.int32, (1, capacity), 1)
    )
    score_scale = 1.0 / math.sqrt(HD)
    saved = []
    for h in range(heads):
        normals = []
        turned = []
        for which in range(2):
            first = which * head_size + h * HD
            normal, scale = normalize(linear[:, first : first + HD])
            normals.append((normal, scale))
            turned.append((normal * cosine + swap_quarters(normal) * sine).astype(jnp.bfloat16))
        first = 2 * head_size + h * HD
        values = linear[:, first : first + HD].astype(jnp.bfloat16)
        queries, keys = turned
        exponent = jnp.where(same, jnp.exp(dot_nt(queries, keys) * score_scale), 0.0)
        prob = exponent / jnp.sum(exponent, axis=1, keepdims=True)
        exponent = jnp.where(same, jnp.exp(dot_nt(keys, queries) * score_scale), 0.0)
        prob_t = exponent / jnp.sum(exponent, axis=0, keepdims=True)
        small[3, 0:capacity, h * HD : (h + 1) * HD] = dot(prob.astype(jnp.bfloat16), values).astype(jnp.bfloat16)
        saved.append((normals, queries, keys, values, prob, prob_t))
    arrivals = [
        across(8, k, 1, small.at[3, pl.ds(0, capacity)], small.at[3, pl.ds(k * capacity, capacity)]) for k in others
    ]

    attn_partial(1)
    transpose_into(slab, gout, gout_in)
    for part in range(2):
        for k in others:
            attn_copies[part, k].wait_recv()
            linear[parts[part], 3 * head_size :] += attn_in[part, k - 1].astype(jnp.float32)

    for h in range(heads):
        normals, queries, keys, values, prob, prob_t = saved[h]
        first = 3 * head_size + h * HD
        grad = linear[:, first : first + HD].astype(jnp.bfloat16)
        grad_prob = dot_nt(grad, values).astype(jnp.bfloat16).astype(jnp.float32)
        grad_score = prob * (grad_prob - jnp.sum(grad_prob * prob, axis=1, keepdims=True)) * score_scale
        grad_prob = dot_nt(values, grad).astype(jnp.bfloat16).astype(jnp.float32)
        grad_score_t = prob_t * (grad_prob - jnp.sum(grad_prob * prob_t, axis=0, keepdims=True)) * score_scale
        gradients = [
            dot(grad_score.astype(jnp.bfloat16), keys),
            dot(grad_score_t.astype(jnp.bfloat16), queries),
        ]
        place = slice(h * HD, (h + 1) * HD)
        for which in range(2):
            gradient = gradients[which].astype(jnp.bfloat16).astype(jnp.float32)
            gradient = gradient * cosine + swap_quarters(gradient * sine)
            small[which, 0:capacity, place] = normalize_back(gradient, *normals[which]).astype(jnp.bfloat16)
        small[2, 0:capacity, place] = dot(prob_t.astype(jnp.bfloat16), grad).astype(jnp.bfloat16)
    arrivals += [
        across(
            9, k, 1, small.at[pl.ds(0, 3), pl.ds(0, capacity)], small.at[pl.ds(0, 3), pl.ds(k * capacity, capacity)]
        )
        for k in others
    ]

    def slice_gradient(first, count, store):
        @pl.loop(0, slab // TILE)
        def tile(t):
            at = pl.ds(pl.multiple_of(t * TILE, TILE), TILE)
            total = sum(dot_nt(small[i, first : first + count, :], weights[i, at, :]) for i in range(3))
            store(at, total.astype(jnp.bfloat16))

    def own_slice(at, value):
        back[shard, :, at] = value

    slice_gradient(0, capacity, own_slice)
    for copy in arrivals:
        copy.wait_recv()

    back_copies = []

    def return_gradients():
        def keep(at, value):
            back_send[:, at] = value

        slice_gradient(capacity, (shards - 1) * capacity, keep)
        for k in others:
            own = pl.ds((k - 1) * capacity, capacity)
            back_copies.append(across(10, k, -1, back_send.at[own], back.at[shard]))

    def token_gradients(number):
        if number == 0:
            for copy in back_copies:
                copy.wait_recv()

        @pl.loop(0, chunk // 2 // group)
        def piece(t):
            at = pl.ds(pl.multiple_of(number * (chunk // 2) + t * group, group), group)
            scale = scale_ref[at, 0:1]
            normal = (tokens_ref[at, :].astype(jnp.float32) - mean_ref[at, 0:1]) * scale
            grad = jnp.concatenate([back[p, at, :] for p in range(shards)], axis=1).astype(jnp.float32)
            tokens_out[at, :] = normalize_back(grad, normal, scale).astype(jnp.bfloat16)

    def term(stream, row):
        row = stream * rows + row
        weight = row // slab
        left = pl.multiple_of((weight // 3) * slab + row % slab, TILE)
        return dot(lhs_ref[pl.ds(left, TILE), :], small[weight])

    def exchange(phase, stream, step, source, target):
        copy = pltpu.make_async_remote_copy(
            src_ref=source,
            dst_ref=target,
            send_sem=send_sem.at[phase, stream, step],
            recv_sem=recv_sem.at[phase, stream, step],
            device_id={"dp": peer_of[orders[stream][step] if step < steps else 0]},
            device_id_type=pl.DeviceIdType.MESH,
        )
        copy.start()
        return copy

    copies = {}
    offsets = {}
    early = [item[1] for item in plan[: next(n for n, item in enumerate(plan) if item[0] == "wait")]]

    def start_first(stream):
        place = pl.ds(0, halves[0])
        copies[0, stream, 0] = exchange(0, stream, 0, outgoing.at[stream, place], incoming.at[stream, place])

    for stream in range(streams):
        half = halves[0]
        mine = bit_of[orders[stream][0]]

        @pl.loop(0, half // TILE)
        def leaving(t):
            value = term(stream, (1 - mine) * half + t * TILE)
            outgoing[stream, pl.ds(pl.multiple_of(t * TILE, TILE), TILE), :] = value.astype(jnp.bfloat16)

        if stream in early:
            start_first(stream)
        offsets[stream, 0] = mine * half

    def first_kept(stream):
        half = halves[0]
        mine = bit_of[orders[stream][0]]

        @pl.loop(0, half // TILE)
        def kept(t):
            acc[stream, pl.ds(pl.multiple_of(t * TILE, TILE), TILE), :] = term(stream, mine * half + t * TILE)

    def combine(stream, step):
        copies[0, stream, step - 1].wait_recv()
        got = starts[step - 1]
        base = offsets[stream, step - 1] - offsets[stream, 0]
        if step == steps:
            half = halves[steps - 1]
            place = pl.ds(pl.multiple_of((core * streams + stream) * rows + offsets[stream, steps - 1], half), half)
            value = acc[stream, pl.ds(pl.multiple_of(base, half), half), :]
            other = incoming[stream, pl.ds(got, half), :]
            out_ref[place, :] = (value + other.astype(jnp.float32)).astype(jnp.bfloat16)
            return
        half = halves[step]
        size = min(half, 192)
        mine = bit_of[orders[stream][step]]
        go, stay = (1 - mine) * half, mine * half

        @pl.loop(0, half // size)
        def leaving(t):
            at = pl.multiple_of(t * size, size)
            value = acc[stream, pl.ds(pl.multiple_of(base + go + at, size), size), :]
            other = incoming[stream, pl.ds(pl.multiple_of(got + go + at, size), size), :]
            outgoing[stream, pl.ds(pl.multiple_of(starts[step] + at, size), size), :] = (
                value + other.astype(jnp.float32)
            ).astype(jnp.bfloat16)

        offsets[stream, step] = offsets[stream, step - 1] + stay

    def combine_kept(stream, step):
        got = starts[step - 1]
        base = offsets[stream, step - 1] - offsets[stream, 0]
        half = halves[step]
        size = min(half, 192)
        stay = bit_of[orders[stream][step]] * half

        @pl.loop(0, half // size)
        def kept(t):
            at = pl.multiple_of(t * size, size)
            where = pl.ds(pl.multiple_of(base + stay + at, size), size)
            other = incoming[stream, pl.ds(pl.multiple_of(got + stay + at, size), size), :]
            acc[stream, where, :] = acc[stream, where, :] + other.astype(jnp.float32)

    return_gradients()
    finish = plan[-1][-1]
    pieces = [(0.5 + 0.1 * number) * finish for number in range(4)]
    behind = []
    for action, stream, phase, step, when in plan:
        if action == "start":
            if phase == 0 and step == 0:
                if stream not in early:
                    start_first(stream)
                continue
            if phase == 0:
                place = pl.ds(starts[step], halves[step])
                source, target = outgoing.at[stream, place], incoming.at[stream, place]
            else:
                size = halves[step] if step < steps else rows
                shift = offsets[stream, step] if step < steps else 0
                place = pl.ds(pl.multiple_of((core * streams + stream) * rows + shift, size), size)
                source, target = out_ref.at[place], out_ref.at[place]
            copies[phase, stream, step] = exchange(phase, stream, step, source, target)
        else:
            for job in behind:
                combine_kept(*job)
            behind = []
            while pieces and when > pieces[0]:
                token_gradients(4 - len(pieces))
                pieces.pop(0)
            if phase == 0:
                if step == 0:
                    first_kept(stream)
                combine(stream, step + 1)
                if step + 1 < steps:
                    behind.append((stream, step + 1))
            else:
                copies[phase, stream, step].wait_recv()
    for copy in copies.values():
        copy.wait_send()
    for copy in started:
        copy.wait_send()


def per_device(tokens, cotangent, lengths, positions, weights):
    capacity, width = tokens.shape
    slab, head_size = weights.shape[1] // CORES, weights.shape[2]
    shards = lax.axis_size("fsdp") * CORES
    steps = lax.axis_size("dp").bit_length() - 2
    streams = next(n for n in (8, 4, 2, 1) if (4 * slab // n >> steps) % 16 == 0)
    rows = 4 * slab // streams
    plain = list(range(1, steps + 1))
    turned = plain[1:] + plain[:1]
    orders = [turned] * (streams // 8) + [plain] * (streams - streams // 8)
    moved = rows - (rows >> steps)
    chunk = capacity // 2
    vmem = pl.BlockSpec(memory_space=pltpu.VMEM)
    half = jnp.bfloat16
    summed, grad_tokens = pl.pallas_call(
        functools.partial(layer_kernel, orders),
        out_shape=(
            jax.ShapeDtypeStruct((CORES * 4 * slab, head_size), half),
            jax.ShapeDtypeStruct((capacity, width), half),
        ),
        in_specs=[vmem, vmem, pl.BlockSpec(memory_space=pltpu.SMEM), vmem, pl.BlockSpec(memory_space=pl.ANY)],
        out_specs=(vmem, vmem),
        scratch_shapes=[
            pltpu.VMEM((4, slab, head_size), half),
            pltpu.VMEM((shards, capacity, slab), half),
            pltpu.VMEM((shards, capacity, slab), half),
            pltpu.VMEM((2, shards - 1, chunk, slab), half),
            pltpu.VMEM((2, shards - 1, chunk, slab), half),
            pltpu.VMEM((capacity, HD), jnp.float32),
            pltpu.VMEM((capacity, HD), jnp.float32),
            pltpu.VMEM((capacity, 4 * head_size), jnp.float32),
            pltpu.VMEM((2, shards - 1, chunk, 3 * head_size), half),
            pltpu.VMEM((2, shards - 1, chunk, 3 * head_size), half),
            pltpu.VMEM((2, shards - 1, chunk, head_size), half),
            pltpu.VMEM((2, shards - 1, chunk, head_size), half),
            pltpu.VMEM((2 * slab, shards * capacity), half),
            pltpu.VMEM((4, shards * capacity, head_size), half),
            pltpu.VMEM((shards, capacity, slab), half),
            pltpu.VMEM(((shards - 1) * capacity, slab), half),
            pltpu.VMEM((streams, rows // 2, head_size), jnp.float32),
            pltpu.VMEM((streams, moved, head_size), half),
            pltpu.VMEM((streams, moved, head_size), half),
            pltpu.SemaphoreType.DMA,
            pltpu.SemaphoreType.DMA((11, shards)),
            pltpu.SemaphoreType.DMA((11, shards)),
            pltpu.SemaphoreType.DMA((2, streams, steps + 1)),
            pltpu.SemaphoreType.DMA((2, streams, steps + 1)),
        ],
        compiler_params=pltpu.CompilerParams(
            collective_id=0, has_side_effects=True, vmem_limit_bytes=62 * 1024 * 1024
        ),
        cost_estimate=pl.CostEstimate(flops=4 * 10**9, bytes_accessed=10**8, transcendentals=10**5),
    )(tokens, cotangent, lengths, positions, weights)
    halved = summed.reshape(CORES, 4, slab, head_size).astype(jnp.float32)
    return (grad_tokens, jnp.transpose(halved, (1, 0, 2, 3)).reshape(weights.shape))


def solution(mesh):
    return jax.shard_map(
        per_device,
        mesh=mesh,
        in_specs=(
            P(("dp", "fsdp"), None),
            P(("dp", "fsdp"), None),
            P(("dp", "fsdp"), None),
            P(None, ("dp", "fsdp")),
            P(None, "fsdp", None),
        ),
        out_specs=(P(("dp", "fsdp"), None), P(None, "fsdp", None)),
        check_vma=False,
    )
```

```python
import functools
import math

import jax
import jax.numpy as jnp
from jax import lax
from jax.experimental import pallas as pl
from jax.experimental.pallas import tpu as pltpu
from jax.sharding import PartitionSpec as P

HD = 128
TILE = 384
CORES = 2

EPS = 1e-06
rope_base = 100.0


def segment_slots(lengths_ref, rows):
    end = 0
    slot = jnp.zeros(rows.shape, jnp.float32)
    for image in range(3):
        end = end + lengths_ref[0, image]
        slot = slot + jnp.where(rows >= end, 1.0, 0.0)
    return jnp.where(slot < 3.0, slot, -1.0)


def rotary_tables(positions_ref):
    capacity = positions_ref.shape[1]
    down = lax.broadcasted_iota(jnp.int32, (capacity, capacity), 0)
    along = lax.broadcasted_iota(jnp.int32, (capacity, capacity), 1)

    def column(i):
        line = positions_ref[i : i + 1, :].astype(jnp.float32)
        return jnp.sum(jnp.where(down == along, line, 0.0), axis=1, keepdims=True)

    lane = lax.broadcasted_iota(jnp.int32, (capacity, HD), 1)
    quarter = HD // 4
    frequency = jnp.exp((lane % quarter).astype(jnp.float32) * (-math.log(rope_base) / quarter))
    angles = jnp.where(lane < HD // 2, column(0), column(1)) * frequency
    sign = jnp.where((lane // quarter) % 2 == 0, -1.0, 1.0)
    return jnp.cos(angles), sign * jnp.sin(angles)


def exchange_plan(orders, halves):
    streams, steps = len(orders), len(halves)
    stages = [(0, s) for s in range(steps)] + [(1, s) for s in reversed(range(steps))] + [(1, steps)]
    busy, flying, waiting = [0.0] * 4, [0] * 4, [[], [], [], []]
    price = [0.25, 1.0, 1.0, 2.0]
    events, plan = [], []

    def launch(now, stream, place):
        step = stages[place][1]
        kind = min(orders[stream][step], 3) if step < steps else 0
        if flying[kind] >= 3:
            waiting[kind].append((stream, place))
            return
        flying[kind] += 1
        size = halves[step] if step < steps else 2 * halves[0]
        busy[kind] = max(busy[kind], now) + size * 0.0114 * price[kind]
        events.append((busy[kind] + 1.0, stream, place, kind))
        plan.append(("start", stream) + stages[place] + (now,))

    for stream in range(streams):
        launch(0.7 * stream, stream, 0)
    now = 0.0
    while events:
        event = min(events)
        events.remove(event)
        when, stream, place, kind = event
        now = max(now + 0.3, when)
        plan.append(("wait", stream) + stages[place] + (now,))
        flying[kind] -= 1
        if waiting[kind]:
            launch(now, *waiting[kind].pop(0))
        if place + 1 < len(stages):
            launch(now, stream, place + 1)
    return plan


def normalize(values):
    center = values - jnp.mean(values, axis=-1, keepdims=True)
    scale = lax.rsqrt(jnp.mean(center * center, axis=-1, keepdims=True) + EPS)
    return center * scale, scale


def normalize_back(grad, normal, scale):
    inner = jnp.mean(grad * normal, axis=-1, keepdims=True)
    return scale * (grad - jnp.mean(grad, axis=-1, keepdims=True) - normal * inner)


def swap_quarters(values):
    quarter = HD // 4
    lane = lax.broadcasted_iota(jnp.int32, values.shape, 1)
    return jnp.where(
        (lane // quarter) % 2 == 0, pltpu.roll(values, HD - quarter, 1), pltpu.roll(values, quarter, 1)
    )


def dot(left, right):
    return jnp.dot(left, right, preferred_element_type=jnp.float32)


def dot_nt(left, right):
    return lax.dot_general(left, right, (((1,), (1,)), ((), ())), preferred_element_type=jnp.float32)


def layer_kernel(
    orders, tokens_ref, cot_ref, lengths_ref, positions_ref, weights_hbm, out_ref, tokens_out,
    weights, normed, gout, norm_in, gout_in, mean_ref, scale_ref, linear, lin_send, lin_in, attn_send, attn_in,
    lhs_ref, small, back, back_send, acc, outgoing, incoming, w_sem, y_send, y_recv, send_sem, recv_sem,
):
    capacity = tokens_ref.shape[0]
    slab, head_size = weights.shape[1], weights.shape[2]
    shards = normed.shape[0]
    heads = head_size // HD
    me = lax.axis_index("dp")
    core = me % CORES
    shard = lax.axis_index("fsdp") * CORES + core
    streams, steps = len(orders), len(orders[0])
    rows = 4 * slab // streams
    halves = [rows >> (s + 1) for s in range(steps)]
    starts = [rows - 2 * halves[s] for s in range(steps)]
    bit_of = [(me // (1 << bit)) % 2 for bit in range(steps + 1)]
    peer_of = [me + (1 - 2 * bit_of[bit]) * (1 << bit) for bit in range(steps + 1)]
    others = range(1, shards)
    plan = exchange_plan(orders, halves)

    def member(offset):
        index = (shard + shards + offset) % shards
        return {"dp": me - core + index % CORES, "fsdp": index // CORES}

    fetch = pltpu.make_async_copy(weights_hbm.at[:, pl.ds(pl.multiple_of(core * slab, slab), slab)], weights, w_sem)
    fetch.start()
    barrier = pltpu.get_barrier_semaphore()
    for bit in range(1, steps + 1):
        pl.semaphore_signal(barrier, inc=1, device_id={"dp": peer_of[bit]}, device_id_type=pl.DeviceIdType.MESH)
    for k in others:
        pl.semaphore_signal(barrier, inc=1, device_id=member(k), device_id_type=pl.DeviceIdType.MESH)

    started = []

    def across(kind, k, direction, source, target):
        copy = pltpu.make_async_remote_copy(
            src_ref=source,
            dst_ref=target,
            send_sem=y_send.at[kind, k],
            recv_sem=y_recv.at[kind, k],
            device_id=member(direction * k),
            device_id_type=pl.DeviceIdType.MESH,
        )
        copy.start()
        started.append(copy)
        return copy

    chunk = capacity // 2
    parts = [pl.ds(0, chunk), pl.ds(chunk, chunk)]
    group = 16

    def mask_cotangent(part):
        @pl.loop(0, chunk // group)
        def masked(t):
            at = pl.ds(pl.multiple_of(part * chunk + t * group, group), group)
            row = part * chunk + t * group + lax.broadcasted_iota(jnp.int32, (group, 1), 0)
            live = jnp.where(segment_slots(lengths_ref, row) >= 0.0, 1.0, 0.0)
            for p in range(shards):
                value = cot_ref[at, p * slab : (p + 1) * slab].astype(jnp.float32)
                gout[p, at, :] = (value * live).astype(jnp.bfloat16)

    def normalize_tokens(part):
        @pl.loop(0, chunk // group)
        def normal(t):
            at = pl.ds(pl.multiple_of(part * chunk + t * group, group), group)
            value = tokens_ref[at, :].astype(jnp.float32)
            mean = jnp.mean(value, axis=-1, keepdims=True)
            center = value - mean
            scale = lax.rsqrt(jnp.mean(center * center, axis=-1, keepdims=True) + EPS)
            mean_ref[at, :] = jnp.broadcast_to(mean, (group, HD))
            scale_ref[at, :] = jnp.broadcast_to(scale, (group, HD))
            result = (center * scale).astype(jnp.bfloat16)
            for p in range(shards):
                normed[p, at, :] = result[:, p * slab : (p + 1) * slab]

    gout_copies, norm_copies = {}, {}

    def send_gout(part):
        for k in others:
            gout_copies[part, k] = across(
                part, k, 1, gout.at[(shard + k) % shards, parts[part]], gout_in.at[part, k - 1]
            )

    def send_norm(part):
        for k in others:
            norm_copies[part, k] = across(
                2 + part, k, 1, normed.at[(shard + k) % shards, parts[part]], norm_in.at[part, k - 1]
            )

    mask_cotangent(0)
    pl.semaphore_wait(barrier, steps + shards - 1)
    send_gout(0)
    normalize_tokens(0)
    send_norm(0)
    normalize_tokens(1)
    send_norm(1)
    mask_cotangent(1)
    send_gout(1)

    fetch.wait()
    for i in range(3):
        linear[:, i * head_size : (i + 1) * head_size] = dot(normed[shard], weights[i])
    linear[:, 3 * head_size :] = dot(gout[shard], weights[3])

    cosine, sine = rotary_tables(positions_ref)
    lin_copies, attn_copies = {}, {}

    apart = (shards - 1, chunk, -1)
    joined = ((shards - 1) * chunk, slab)

    def attn_partial(part):
        for k in others:
            gout_copies[part, k].wait_recv()
        partial = dot(gout_in[part].reshape(joined), weights[3])
        attn_send[part] = partial.astype(jnp.bfloat16).reshape(apart)
        for k in others:
            attn_copies[part, k] = across(4 + part, k, -1, attn_send.at[part, k - 1], attn_in.at[part, k - 1])

    def lin_partial(part):
        for k in others:
            norm_copies[part, k].wait_recv()
        for i in range(3):
            partial = dot(norm_in[part].reshape(joined), weights[i])
            lin_send[part, :, :, i * head_size : (i + 1) * head_size] = partial.astype(jnp.bfloat16).reshape(apart)
        for k in others:
            lin_copies[part, k] = across(6 + part, k, -1, lin_send.at[part, k - 1], lin_in.at[part, k - 1])

    attn_partial(0)
    lin_partial(0)
    lin_partial(1)

    def transpose_into(base, own, arrived):
        @pl.loop(0, slab // TILE)
        def turn(t):
            at = pl.ds(pl.multiple_of(t * TILE, TILE), TILE)
            whole = jnp.concatenate([own[shard, :, at]] + [arrived[part, k - 1, :, at] for k in others for part in range(2)], axis=0)
            lhs_ref[pl.ds(pl.multiple_of(base + t * TILE, TILE), TILE), :] = whole.T

    transpose_into(0, normed, norm_in)
    for part in range(2):
        for k in others:
            lin_copies[part, k].wait_recv()
            linear[parts[part], : 3 * head_size] += lin_in[part, k - 1].astype(jnp.float32)

    same = segment_slots(lengths_ref, lax.broadcasted_iota(jnp.int32, (capacity, 1), 0)) == segment_slots(
        lengths_ref, lax.broadcasted_iota(jnp.int32, (1, capacity), 1)
    )
    score_scale = 1.0 / math.sqrt(HD)
    saved = []
    for h in range(heads):
        normals = []
        turned = []
        for which in range(2):
            first = which * head_size + h * HD
            normal, scale = normalize(linear[:, first : first + HD])
            normals.append((normal, scale))
            turned.append((normal * cosine + swap_quarters(normal) * sine).astype(jnp.bfloat16))
        first = 2 * head_size + h * HD
        values = linear[:, first : first + HD].astype(jnp.bfloat16)
        queries, keys = turned
        exponent = jnp.where(same, jnp.exp(dot_nt(queries, keys) * score_scale), 0.0)
        prob = exponent / jnp.sum(exponent, axis=1, keepdims=True)
        exponent = jnp.where(same, jnp.exp(dot_nt(keys, queries) * score_scale), 0.0)
        prob_t = exponent / jnp.sum(exponent, axis=0, keepdims=True)
        small[3, 0:capacity, h * HD : (h + 1) * HD] = dot(prob.astype(jnp.bfloat16), values).astype(jnp.bfloat16)
        saved.append((normals, queries, keys, values, prob, prob_t))
    arrivals = [
        across(8, k, 1, small.at[3, pl.ds(0, capacity)], small.at[3, pl.ds(k * capacity, capacity)]) for k in others
    ]

    attn_partial(1)
    transpose_into(slab, gout, gout_in)
    for part in range(2):
        for k in others:
            attn_copies[part, k].wait_recv()
            linear[parts[part], 3 * head_size :] += attn_in[part, k - 1].astype(jnp.float32)

    for h in range(heads):
        normals, queries, keys, values, prob, prob_t = saved[h]
        first = 3 * head_size + h * HD
        grad = linear[:, first : first + HD].astype(jnp.bfloat16)
        grad_prob = dot_nt(grad, values).astype(jnp.bfloat16).astype(jnp.float32)
        grad_score = prob * (grad_prob - jnp.sum(grad_prob * prob, axis=1, keepdims=True)) * score_scale
        grad_prob = dot_nt(values, grad).astype(jnp.bfloat16).astype(jnp.float32)
        grad_score_t = prob_t * (grad_prob - jnp.sum(grad_prob * prob_t, axis=0, keepdims=True)) * score_scale
        gradients = [
            dot(grad_score.astype(jnp.bfloat16), keys),
            dot(grad_score_t.astype(jnp.bfloat16), queries),
        ]
        place = slice(h * HD, (h + 1) * HD)
        for which in range(2):
            gradient = gradients[which].astype(jnp.bfloat16).astype(jnp.float32)
            gradient = gradient * cosine + swap_quarters(gradient * sine)
            small[which, 0:capacity, place] = normalize_back(gradient, *normals[which]).astype(jnp.bfloat16)
        small[2, 0:capacity, place] = dot(prob_t.astype(jnp.bfloat16), grad).astype(jnp.bfloat16)
    arrivals += [
        across(
            9, k, 1, small.at[pl.ds(0, 3), pl.ds(0, capacity)], small.at[pl.ds(0, 3), pl.ds(k * capacity, capacity)]
        )
        for k in others
    ]

    def slice_gradient(first, count, store):
        @pl.loop(0, slab // TILE)
        def tile(t):
            at = pl.ds(pl.multiple_of(t * TILE, TILE), TILE)
            total = sum(dot_nt(small[i, first : first + count, :], weights[i, at, :]) for i in range(3))
            store(at, total.astype(jnp.bfloat16))

    def own_slice(at, value):
        back[shard, :, at] = value

    slice_gradient(0, capacity, own_slice)
    for copy in arrivals:
        copy.wait_recv()

    back_copies = []

    def return_gradients():
        def keep(at, value):
            back_send[:, at] = value

        slice_gradient(capacity, (shards - 1) * capacity, keep)
        for k in others:
            own = pl.ds((k - 1) * capacity, capacity)
            back_copies.append(across(10, k, -1, back_send.at[own], back.at[shard]))

    def token_gradients(number):
        if number == 0:
            for copy in back_copies:
                copy.wait_recv()

        @pl.loop(0, chunk // 2 // group)
        def piece(t):
            at = pl.ds(pl.multiple_of(number * (chunk // 2) + t * group, group), group)
            scale = scale_ref[at, 0:1]
            normal = (tokens_ref[at, :].astype(jnp.float32) - mean_ref[at, 0:1]) * scale
            grad = jnp.concatenate([back[p, at, :] for p in range(shards)], axis=1).astype(jnp.float32)
            tokens_out[at, :] = normalize_back(grad, normal, scale).astype(jnp.bfloat16)

    def term(stream, row):
        row = stream * rows + row
        weight = row // slab
        left = pl.multiple_of((weight // 3) * slab + row % slab, TILE)
        return dot(lhs_ref[pl.ds(left, TILE), :], small[weight])

    def exchange(phase, stream, step, source, target):
        copy = pltpu.make_async_remote_copy(
            src_ref=source,
            dst_ref=target,
            send_sem=send_sem.at[phase, stream, step],
            recv_sem=recv_sem.at[phase, stream, step],
            device_id={"dp": peer_of[orders[stream][step] if step < steps else 0]},
            device_id_type=pl.DeviceIdType.MESH,
        )
        copy.start()
        return copy

    copies = {}
    offsets = {}
    early = [item[1] for item in plan[: next(n for n, item in enumerate(plan) if item[0] == "wait")]]

    def start_first(stream):
        place = pl.ds(0, halves[0])
        copies[0, stream, 0] = exchange(0, stream, 0, outgoing.at[stream, place], incoming.at[stream, place])

    for stream in range(streams):
        half = halves[0]
        mine = bit_of[orders[stream][0]]

        @pl.loop(0, half // TILE)
        def leaving(t):
            value = term(stream, (1 - mine) * half + t * TILE)
            outgoing[stream, pl.ds(pl.multiple_of(t * TILE, TILE), TILE), :] = value.astype(jnp.bfloat16)

        if stream in early:
            start_first(stream)
        offsets[stream, 0] = mine * half

    def first_kept(stream):
        half = halves[0]
        mine = bit_of[orders[stream][0]]

        @pl.loop(0, half // TILE)
        def kept(t):
            acc[stream, pl.ds(pl.multiple_of(t * TILE, TILE), TILE), :] = term(stream, mine * half + t * TILE)

    def placed(stream, shift):
        if rows > slab:
            return (core * streams + stream) * rows + shift
        weight = stream * rows // slab
        return (weight * CORES + core) * slab + stream * rows % slab + shift

    def combine(stream, step):
        copies[0, stream, step - 1].wait_recv()
        got = starts[step - 1]
        base = offsets[stream, step - 1] - offsets[stream, 0]
        if step == steps:
            half = halves[steps - 1]
            place = pl.ds(pl.multiple_of(placed(stream, offsets[stream, steps - 1]), half), half)
            value = acc[stream, pl.ds(pl.multiple_of(base, half), half), :]
            other = incoming[stream, pl.ds(got, half), :]
            out_ref[place, :] = (value + other.astype(jnp.float32)).astype(jnp.bfloat16)
            return
        half = halves[step]
        size = min(half, 192)
        mine = bit_of[orders[stream][step]]
        go, stay = (1 - mine) * half, mine * half

        @pl.loop(0, half // size)
        def leaving(t):
            at = pl.multiple_of(t * size, size)
            value = acc[stream, pl.ds(pl.multiple_of(base + go + at, size), size), :]
            other = incoming[stream, pl.ds(pl.multiple_of(got + go + at, size), size), :]
            outgoing[stream, pl.ds(pl.multiple_of(starts[step] + at, size), size), :] = (
                value + other.astype(jnp.float32)
            ).astype(jnp.bfloat16)

        offsets[stream, step] = offsets[stream, step - 1] + stay

    def combine_kept(stream, step):
        got = starts[step - 1]
        base = offsets[stream, step - 1] - offsets[stream, 0]
        half = halves[step]
        size = min(half, 192)
        stay = bit_of[orders[stream][step]] * half

        @pl.loop(0, half // size)
        def kept(t):
            at = pl.multiple_of(t * size, size)
            where = pl.ds(pl.multiple_of(base + stay + at, size), size)
            other = incoming[stream, pl.ds(pl.multiple_of(got + stay + at, size), size), :]
            acc[stream, where, :] = acc[stream, where, :] + other.astype(jnp.float32)

    return_gradients()
    finish = plan[-1][-1]
    pieces = [(0.5 + 0.1 * number) * finish for number in range(4)]
    behind = []
    for action, stream, phase, step, when in plan:
        if action == "start":
            if phase == 0 and step == 0:
                if stream not in early:
                    start_first(stream)
                continue
            if phase == 0:
                place = pl.ds(starts[step], halves[step])
                source, target = outgoing.at[stream, place], incoming.at[stream, place]
            else:
                size = halves[step] if step < steps else rows
                shift = offsets[stream, step] if step < steps else 0
                place = pl.ds(pl.multiple_of(placed(stream, shift), size), size)
                source, target = out_ref.at[place], out_ref.at[place]
            copies[phase, stream, step] = exchange(phase, stream, step, source, target)
        else:
            for job in behind:
                combine_kept(*job)
            behind = []
            while pieces and when > pieces[0]:
                token_gradients(4 - len(pieces))
                pieces.pop(0)
            if phase == 0:
                if step == 0:
                    first_kept(stream)
                combine(stream, step + 1)
                if step + 1 < steps:
                    behind.append((stream, step + 1))
            else:
                copies[phase, stream, step].wait_recv()
    for copy in copies.values():
        copy.wait_send()
    for copy in started:
        copy.wait_send()


def per_device(tokens, cotangent, lengths, positions, weights):
    capacity, width = tokens.shape
    slab, head_size = weights.shape[1] // CORES, weights.shape[2]
    shards = lax.axis_size("fsdp") * CORES
    steps = lax.axis_size("dp").bit_length() - 2
    streams = next(n for n in (8, 4, 2, 1) if (4 * slab // n >> steps) % 16 == 0)
    rows = 4 * slab // streams
    plain = list(range(1, steps + 1))
    turned = plain[1:] + plain[:1]
    orders = [turned] * (streams // 8) + [plain] * (streams - streams // 8)
    moved = rows - (rows >> steps)
    chunk = capacity // 2
    vmem = pl.BlockSpec(memory_space=pltpu.VMEM)
    half = jnp.bfloat16
    summed, grad_tokens = pl.pallas_call(
        functools.partial(layer_kernel, orders),
        out_shape=(
            jax.ShapeDtypeStruct((CORES * 4 * slab, head_size), half),
            jax.ShapeDtypeStruct((capacity, width), half),
        ),
        in_specs=[vmem, vmem, pl.BlockSpec(memory_space=pltpu.SMEM), vmem, pl.BlockSpec(memory_space=pl.ANY)],
        out_specs=(vmem, vmem),
        scratch_shapes=[
            pltpu.VMEM((4, slab, head_size), half),
            pltpu.VMEM((shards, capacity, slab), half),
            pltpu.VMEM((shards, capacity, slab), half),
            pltpu.VMEM((2, shards - 1, chunk, slab), half),
            pltpu.VMEM((2, shards - 1, chunk, slab), half),
            pltpu.VMEM((capacity, HD), jnp.float32),
            pltpu.VMEM((capacity, HD), jnp.float32),
            pltpu.VMEM((capacity, 4 * head_size), jnp.float32),
            pltpu.VMEM((2, shards - 1, chunk, 3 * head_size), half),
            pltpu.VMEM((2, shards - 1, chunk, 3 * head_size), half),
            pltpu.VMEM((2, shards - 1, chunk, head_size), half),
            pltpu.VMEM((2, shards - 1, chunk, head_size), half),
            pltpu.VMEM((2 * slab, shards * capacity), half),
            pltpu.VMEM((4, shards * capacity, head_size), half),
            pltpu.VMEM((shards, capacity, slab), half),
            pltpu.VMEM(((shards - 1) * capacity, slab), half),
            pltpu.VMEM((streams, rows // 2, head_size), jnp.float32),
            pltpu.VMEM((streams, moved, head_size), half),
            pltpu.VMEM((streams, moved, head_size), half),
            pltpu.SemaphoreType.DMA,
            pltpu.SemaphoreType.DMA((11, shards)),
            pltpu.SemaphoreType.DMA((11, shards)),
            pltpu.SemaphoreType.DMA((2, streams, steps + 1)),
            pltpu.SemaphoreType.DMA((2, streams, steps + 1)),
        ],
        compiler_params=pltpu.CompilerParams(
            collective_id=0, has_side_effects=True, vmem_limit_bytes=62 * 1024 * 1024
        ),
        cost_estimate=pl.CostEstimate(flops=4 * 10**9, bytes_accessed=10**8, transcendentals=10**5),
    )(tokens, cotangent, lengths, positions, weights)
    if rows > slab:
        summed = jnp.transpose(summed.reshape(CORES, 4, slab, head_size), (1, 0, 2, 3))
    return (grad_tokens, summed.reshape(weights.shape).astype(jnp.float32))


def solution(mesh):
    return jax.shard_map(
        per_device,
        mesh=mesh,
        in_specs=(
            P(("dp", "fsdp"), None),
            P(("dp", "fsdp"), None),
            P(("dp", "fsdp"), None),
            P(None, ("dp", "fsdp")),
            P(None, "fsdp", None),
        ),
        out_specs=(P(("dp", "fsdp"), None), P(None, "fsdp", None)),
        check_vma=False,
    )
```
